32 devices in a mesh: fsdp: 32 (over z, y, x, core).
Axes of the slice: x: 2, y: 2, z: 4, core: 2. Of those that a mesh axis runs over, the one named last changes fastest.
Arguments:
- images: bfloat16 [32, 197, 768], P('fsdp'), may hold values from -10.5 to 10.5
- slots: int32 [32, 3, 136], P('fsdp'), may hold values from -1 to 393, as said below
- small_params: bfloat16 [6144], P('fsdp'), may hold values from -0.3 to 1.4
- qkv_weight: bfloat16 [1769472], P('fsdp'), may hold values from -0.21875 to 0.21875
- out_weight: bfloat16 [589824], P('fsdp'), may hold values from -0.875 to 0.875
- expert_in: bfloat16 [7077888], P('fsdp'), may hold values from -0.21875 to 0.21875
- expert_out: bfloat16 [7077888], P('fsdp'), may hold values from -0.109375 to 0.109375
- cotangent: bfloat16 [32, 197, 768], P('fsdp'), may hold values from -4 to 4
Outputs:
- block_output: bfloat16 [32, 197, 768], P('fsdp')
- input_grad: bfloat16 [32, 197, 768], P('fsdp')
- small_grad: float32 [6144], P('fsdp')
- qkv_weight_grad: float32 [1769472], P('fsdp')
- out_weight_grad: float32 [589824], P('fsdp')
- expert_in_grad: float32 [7077888], P('fsdp')
- expert_out_grad: float32 [7077888], P('fsdp')
The draws below stay inside these ranges and needn't reach their ends.
Inputs may be any that keep to these rules, and one draw needn't show every extreme that they name: Values 2 t + r name token t of the image and its choice r; -1 marks an empty slot, and an expert's empty slots follow its filled ones. Each token of an image appears exactly twice, once with r = 0 and once with r = 1, at two different experts. In every image some expert fills all 136 slots.
All inputs are finite; a program needn't handle non-finite values.
Results may differ from the reference program's by a relative error of at most 0.012.
Values may be sent and summed in bfloat16 or wider, within the bound.
No kernel may reach another device: no remote copies, remote signals or barrier semaphores. Data moves between devices by JAX's collectives and lax.ppermute only.
A program may use at most 320 MiB of HBM per device.

```python
import math
import jax
import jax.numpy as jnp
from jax import lax

D = 768
HEADS = 12
HEAD_DIM = 64
FF = 3072
EXPERTS = 3
GROUP = 4
PATCHES = 197
MIN_PAIR = 61
CAP = 136
IMAGES = 32
FFQ = 768
PIECE = 221184
N_FSDP = 32


def draw_images(key, part):
    key = jax.random.fold_in(key, 3)
    scale_key, value_key = jax.random.split(key, 2)
    row_scale = jnp.exp(jax.random.uniform(scale_key, (IMAGES, PATCHES, 1), jnp.float32, math.log(0.35), math.log(3.5)))
    values = jnp.clip(jax.random.normal(value_key, (IMAGES, PATCHES, D), jnp.float32), -3.0, 3.0) * row_scale
    return jnp.clip(values, -10.5, 10.5).astype(jnp.bfloat16)


def draw_small_params(key, part):
    key = jax.random.fold_in(key, 7)
    keys = jax.random.split(key, 6)
    gain_one = jax.random.uniform(keys[0], (D,), jnp.float32, 0.6, 1.4)
    bias_one = jnp.clip(0.1 * jax.random.normal(keys[1], (D,), jnp.float32), -0.29, 0.29)
    gain_two = jax.random.uniform(keys[2], (D,), jnp.float32, 0.6, 1.4)
    bias_two = jnp.clip(0.1 * jax.random.normal(keys[3], (D,), jnp.float32), -0.29, 0.29)
    bias_out = jnp.clip(0.1 * jax.random.normal(keys[4], (D,), jnp.float32), -0.29, 0.29)
    router = jnp.clip(0.7 / math.sqrt(D) * jax.random.normal(keys[5], (D * EXPERTS,), jnp.float32), -0.29, 0.29)
    return jnp.concatenate([gain_one, bias_one, gain_two, bias_two, bias_out, router]).astype(jnp.bfloat16)


def image_slots(key):
    pair_key, count_key, ordering_key, swapped_key, shuffle_key = jax.random.split(key, 5)
    rarest = jax.random.randint(pair_key, (), 0, 3)
    remaining = PATCHES - MIN_PAIR
    second_count = jax.random.randint(count_key, (), MIN_PAIR, remaining - MIN_PAIR + 1)
    pair_counts = jnp.roll(jnp.stack([jnp.array(MIN_PAIR, jnp.int32), second_count.astype(jnp.int32), (remaining - second_count).astype(jnp.int32)]), rarest)
    positions = jnp.arange(PATCHES, dtype=jnp.int32)
    kind_at = (positions >= pair_counts[0]).astype(jnp.int32) + (positions >= pair_counts[0] + pair_counts[1]).astype(jnp.int32)
    ordering = jax.random.permutation(ordering_key, PATCHES).astype(jnp.int32)
    pair_kind = jnp.zeros((PATCHES,), jnp.int32).at[ordering].set(kind_at)
    lower_expert = jnp.array([0, 0, 1], jnp.int32)[pair_kind]
    upper_expert = jnp.array([1, 2, 2], jnp.int32)[pair_kind]
    swapped = jax.random.randint(swapped_key, (PATCHES,), 0, 2)
    first_choice = jnp.where(swapped == 1, upper_expert, lower_expert)
    second_choice = jnp.where(swapped == 1, lower_expert, upper_expert)
    shuffle = jax.random.permutation(shuffle_key, PATCHES).astype(jnp.int32)

    def expert_slots(expert):
        rank_one = second_choice == expert
        belongs = (first_choice == expert) | rank_one
        ranking = jnp.where(belongs, shuffle, PATCHES + positions)
        selected = jnp.argsort(ranking, stable=True)[:CAP].astype(jnp.int32)
        return jnp.where(belongs[selected], 2 * selected + rank_one[selected].astype(jnp.int32), -1)
    return jax.vmap(expert_slots)(jnp.arange(EXPERTS, dtype=jnp.int32))


def draw_slots(key, part):
    key = jax.random.fold_in(key, 5)
    return jax.vmap(image_slots)(jax.random.split(key, IMAGES)).astype(jnp.int32)


def block_scale(own_key, shape, pieces, least, high):
    def one(dim, parts):
        heights = jax.random.uniform(jax.random.fold_in(jax.random.fold_in(own_key, 6), dim), (parts,), jnp.float32, least / len(pieces), high / len(pieces))
        return jnp.repeat(jnp.exp(heights), shape[dim] // parts).reshape((-1,) + (1,) * (len(shape) - dim - 1))

    gain = one(*pieces[0])
    for cut in pieces[1:]:
        gain = gain * one(*cut)
    return gain


def normal_values(rng, dims, spread, bound, cuts=(), kind=jnp.bfloat16):
    drawn = spread * jax.random.normal(rng, dims, jnp.float32)
    if cuts:
        drawn = drawn * block_scale(rng, dims, cuts, -0.22, 0.18)
    return jnp.clip(drawn, -bound, bound).astype(kind)


def setup_inputs(seed: int = 0) -> dict:
    seeds = jax.random.split(jax.random.key(seed), 9)
    images = draw_images(jax.random.fold_in(seeds[8], 71), 0)
    slots = draw_slots(jax.random.fold_in(seeds[8], 71), 0)
    small_params = draw_small_params(jax.random.fold_in(seeds[8], 71), 0)
    qkv_weight = normal_values(seeds[3], (3 * D * D,), D ** -0.5, 0.21875, ((0, 32),))
    out_weight = normal_values(seeds[4], (D * D,), (D // 16) ** -0.5, 0.875, ((0, 32),))
    expert_in = normal_values(seeds[5], (EXPERTS * D * FF,), D ** -0.5, 0.21875, ((0, 32),))
    expert_out = normal_values(seeds[6], (EXPERTS * FF * D,), FF ** -0.5, 0.109375, ((0, 32),))
    cotangent = normal_values(seeds[7], (IMAGES, PATCHES, D), 1.0, 4.0, ((0, 32),))
    return {"images": images, "slots": slots, "small_params": small_params, "qkv_weight": qkv_weight, "out_weight": out_weight, "expert_in": expert_in, "expert_out": expert_out, "cotangent": cotangent}


@jax.custom_vjp
def low(v):
    return lax.optimization_barrier(v.astype(jnp.bfloat16)).astype(jnp.float32)

@jax.custom_vjp
def low_back(v):
    return v

def low_keep(v):
    return (low(v), None)

def low_pass(kept, grad):
    return (grad,)

def back_keep(v):
    return (v, None)

def back_low(kept, grad):
    return (low(grad),)
low.defvjp(low_keep, low_pass)
low_back.defvjp(back_keep, back_low)
EPSILON = 1e-06
HIGHEST_PRECISION = lax.Precision.HIGHEST

def round_both(value):
    return low(low_back(value))

def layer_norm(value, weight_gain, weight_bias):
    average = lax.optimization_barrier(jnp.mean(value, axis=-1, keepdims=True))
    centred = value - average
    variance = lax.optimization_barrier(jnp.mean(centred * centred, axis=-1, keepdims=True))
    return centred * lax.rsqrt(variance + EPSILON) * weight_gain + weight_bias

def arrange_first(flat):
    blocks = flat.reshape(N_FSDP // GROUP, GROUP, PIECE).transpose(1, 0, 2)
    return blocks.reshape(GROUP, EXPERTS, D, FFQ).transpose(1, 2, 0, 3).reshape(EXPERTS, D, FF)

def arrange_second(flat):
    blocks = flat.reshape(N_FSDP // GROUP, GROUP, PIECE).transpose(1, 0, 2)
    return blocks.reshape(GROUP, EXPERTS, FFQ, D).transpose(1, 0, 2, 3).reshape(EXPERTS, FF, D)

def pick_rows(source_rows, indices):
    return jax.vmap(lambda table_part, wanted: jnp.take(table_part, wanted, axis=0))(source_rows, indices)

def routing(slot_codes):
    batch_size = slot_codes.shape[0]
    flat_codes = slot_codes.reshape(batch_size, EXPERTS * CAP)
    filled = flat_codes >= 0
    targets = jnp.where(filled, flat_codes, 2 * PATCHES)
    slot_numbers = jnp.broadcast_to(jnp.arange(EXPERTS * CAP, dtype=jnp.int32), flat_codes.shape)

    def place_slots(target_row, number_row):
        return jnp.zeros((2 * PATCHES,), jnp.int32).at[target_row].set(number_row, mode='drop')
    position = jax.vmap(place_slots)(targets, slot_numbers)
    slot_token = jnp.where(filled, flat_codes // 2, 0).astype(jnp.int32)
    return (position, slot_token, filled)

def forward(params, inputs, slot_codes):
    small_full, qkv_flat, out_flat, in_flat, back_flat = params
    gain_one = small_full[0:D]
    bias_one = small_full[D:2 * D]
    gain_two = small_full[2 * D:3 * D]
    bias_two = small_full[3 * D:4 * D]
    bias_out = small_full[4 * D:5 * D]
    router = small_full[5 * D:].reshape(D, EXPERTS)
    batch_size = inputs.shape[0]
    score_scale = 1.0 / math.sqrt(HEAD_DIM)
    first_normed = low(layer_norm(inputs, gain_one, bias_one))
    packed = round_both(jnp.einsum('bsd,de->bse', first_normed, qkv_flat.reshape(D, 3 * D), precision=HIGHEST_PRECISION))
    queries = packed[..., :D].reshape(batch_size, PATCHES, HEADS, HEAD_DIM)
    key_heads = packed[..., D:2 * D].reshape(batch_size, PATCHES, HEADS, HEAD_DIM)
    value_heads = packed[..., 2 * D:].reshape(batch_size, PATCHES, HEADS, HEAD_DIM)
    scores = low_back(jnp.einsum('bqhe,bkhe->bhqk', queries, key_heads, precision=HIGHEST_PRECISION) * score_scale)
    probabilities = low(jax.nn.softmax(scores, axis=-1))
    attended = round_both(jnp.einsum('bhqk,bkhe->bqhe', probabilities, value_heads, precision=HIGHEST_PRECISION).reshape(batch_size, PATCHES, D))
    projected = low_back(jnp.einsum('bsd,de->bse', attended, out_flat.reshape(D, D), precision=HIGHEST_PRECISION))
    middle = inputs + projected + bias_out
    second = low(layer_norm(middle, gain_two, bias_two))
    logits = low_back(jnp.einsum('bsd,de->bse', second, router, precision=HIGHEST_PRECISION))
    position, slot_token, filled = routing(slot_codes)
    expert_of = (position // CAP).reshape(batch_size, PATCHES, 2)
    chosen = jnp.take_along_axis(logits, expert_of, axis=-1)
    gate_weights = jax.nn.softmax(chosen, axis=-1)
    dispatched = pick_rows(second, slot_token) * filled[..., None].astype(jnp.float32)
    dispatched = dispatched.reshape(batch_size, EXPERTS, CAP, D)
    hidden = low_back(jnp.einsum('becd,edf->becf', dispatched, arrange_first(in_flat), precision=HIGHEST_PRECISION))
    active = low(jax.nn.gelu(hidden, approximate=False))
    produced = low_back(jnp.einsum('becf,efd->becd', active, arrange_second(back_flat), precision=HIGHEST_PRECISION))
    gathered_rows = pick_rows(produced.reshape(batch_size, EXPERTS * CAP, D), position)
    mixture = lax.optimization_barrier(jnp.sum(gathered_rows.reshape(batch_size, PATCHES, 2, D) * gate_weights[..., None], axis=2))
    return middle + mixture

def reference(images, slots, small_params, qkv_weight, out_weight, expert_in, expert_out, cotangent):
    params = (small_params.astype(jnp.float32), qkv_weight.astype(jnp.float32), out_weight.astype(jnp.float32), expert_in.astype(jnp.float32), expert_out.astype(jnp.float32))
    group_images = images.astype(jnp.float32).reshape(-1, 8, PATCHES, D)
    group_slots = slots.reshape(-1, 8, EXPERTS, CAP)
    group_cotangent = cotangent.astype(jnp.float32).reshape(-1, 8, PATCHES, D)

    def group_step(totals, group_item):
        block_inputs, block_slots, block_cotangent = group_item
        outputs, pullback = jax.vjp(lambda weights, values: forward(weights, values, block_slots), params, block_inputs)
        weight_grads, inputs_grad = pullback(block_cotangent)
        totals = jax.tree.map(jnp.add, totals, weight_grads)
        return (totals, (outputs.astype(jnp.bfloat16), inputs_grad.astype(jnp.bfloat16)))
    zero_grads = jax.tree.map(jnp.zeros_like, params)
    totals, (outputs, inputs_grad) = lax.scan(group_step, zero_grads, (group_images, group_slots, group_cotangent))
    return (outputs.reshape(IMAGES, PATCHES, D), inputs_grad.reshape(IMAGES, PATCHES, D), totals[0], totals[1], totals[2], totals[3], totals[4])
```

```python
import math

import jax
import jax.numpy as jnp
from jax import lax
from jax.experimental import pallas as pl
from jax.experimental.pallas import tpu as pltpu
from jax.sharding import PartitionSpec as P

D = 768
HEADS = 12
HEAD_DIM = 64
EXPERTS = 3
GROUP = 4
PATCHES = 197
CAP = 136
EPSILON = 1e-06

ZS = 4
TEAM = 32
PIECES = TEAM // GROUP
PIECE_ROWS = EXPERTS * D // PIECES
STEP = 96
REACH = 3
BLOCK = 192
BLOCKS = 3
WIDE = 2 * BLOCK
TOKENS = 208
SLOTS = 144
LANES = 128
HALF = D // 2

f32 = jnp.float32
bf16 = jnp.bfloat16


def norm_forward(value, gain, bias):
    average = jnp.mean(value, axis=-1, keepdims=True)
    centred = value - average
    inverse = lax.rsqrt(jnp.mean(centred * centred, axis=-1, keepdims=True) + EPSILON)
    normed = centred * inverse
    return normed * gain + bias, normed, inverse


def norm_backward(incoming, normed, inverse, gain):
    scaled = incoming * gain
    returned = inverse * (
        scaled
        - jnp.mean(scaled, axis=-1, keepdims=True)
        - normed * jnp.mean(scaled * normed, axis=-1, keepdims=True)
    )
    return returned, jnp.sum(incoming * normed, axis=0), jnp.sum(incoming, axis=0)


def dot(a, b, dims):
    return lax.dot_general(a, b, (dims, ((), ())), preferred_element_type=f32)


NN = ((1,), (0,))
NT = ((1,), (1,))
TN = ((0,), (0,))


class Place:
    def __init__(self):
        self.teams = lax.axis_size("fsdp") // TEAM
        index = lax.axis_index("fsdp")
        self.core = index % 2
        self.x = (index // 2) % 2
        self.piece = index // (GROUP * self.teams)
        self.y = self.piece % 2
        self.z = self.piece // 2

    def index(self, z, y, x, core, team):
        return ((2 * z + y) * self.teams + team) * GROUP + 2 * x + core

    def send(self, value, move):
        pairs = []
        for team in range(self.teams):
            for z in range(ZS):
                for y in range(2):
                    for x in range(2):
                        for core in range(2):
                            to = move(z, y, x, core)
                            if to is not None:
                                pairs.append(
                                    (self.index(z, y, x, core, team), self.index(*to, team))
                                )
        return lax.ppermute(value, "fsdp", pairs)

    def swap_core(self, value):
        return self.send(value, lambda z, y, x, c: (z, y, x, 1 - c))

    def flip(self, value, dy, dx):
        return self.send(value, lambda z, y, x, c: (z, y ^ dy, x ^ dx, c))

    def roll(self, value, k):
        return self.send(value, lambda z, y, x, c: ((z + k) % ZS, y, x, c))

    def shift(self, value, s):
        def move(z, y, x, c):
            to = 2 * z + y + s
            return (to // 2, to % 2, x, c) if 0 <= to < PIECES else None

        return self.send(value, move)

    def plane_groups(self):
        return [
            [self.index(z, y, x, c, team) for y in range(2) for x in range(2)]
            for team in range(self.teams)
            for z in range(ZS)
            for c in range(2)
        ]

    def team_groups(self):
        return [
            [self.index(z, y, x, c, team) for team in range(self.teams)]
            for z in range(ZS)
            for y in range(2)
            for x in range(2)
            for c in range(2)
        ]


def turn(place, piece):
    upright = piece.T
    twice = jnp.concatenate([upright, upright], axis=0)
    parts = []
    for s in range(REACH, -REACH - 1, -1):
        start = (PIECE_ROWS * (place.piece + s + PIECES)) % D
        tile = lax.dynamic_slice(twice, (start, 0), (PIECE_ROWS, PIECE_ROWS))
        parts.append(place.shift(tile, s) if s else tile)
    row = jnp.concatenate(parts, axis=1)
    steps = PIECE_ROWS // STEP
    blocks = []
    for j in range(steps):
        expert = (steps * place.piece + j) // (D // STEP)
        start = STEP * ((D // STEP) * expert - steps * (place.piece - REACH))
        blocks.append(lax.dynamic_slice(row, (STEP * j, start), (STEP, D)))
    return jnp.concatenate(blocks, axis=0)


def block_rows(k):
    low, high = BLOCK * k, BLOCK * (k + 1)
    found = []
    for y in range(2):
        a, b = max(low, PIECE_ROWS * y), min(high, PIECE_ROWS * (y + 1))
        if a < b:
            found.append((y, a - PIECE_ROWS * y, b - PIECE_ROWS * y))
    return found


def pair_kernel(
    expert_ref,
    second_ref,
    dy_ref,
    slots_ref,
    router_ref,
    weight_ref,
    back_ref,
    mix_ref,
    rows_ref,
    grads_ref,
    active_ref,
    hidden_grad_ref,
    back_sum,
    mix_sum,
):
    lane = lax.broadcasted_iota(jnp.int32, (TOKENS, LANES), 1)
    token = lax.broadcasted_iota(jnp.int32, (TOKENS, SLOTS), 0)
    gates = []
    for i in range(2):
        there = jnp.zeros((TOKENS, LANES), f32)
        for e in range(EXPERTS):
            match = (token == slots_ref[i, e : e + 1, :]).astype(f32)
            there = jnp.where(lane == e, jnp.max(match, axis=1, keepdims=True), there)
        logits = dot(second_ref[i], router_ref[...], NN)
        masked = jnp.where(there > 0, logits, -1e30)
        peak = jnp.max(masked, axis=1, keepdims=True)
        weight = jnp.where(there > 0, jnp.exp(masked - peak), 0.0)
        total = jnp.sum(weight, axis=1, keepdims=True)
        gates.append(weight / jnp.where(total > 0, total, 1.0))
    back_sum[...] = jnp.zeros_like(back_sum)
    mix_sum[...] = jnp.zeros_like(mix_sum)
    for k in range(BLOCKS):
        expert = expert_ref[k]
        w_in = jnp.concatenate(
            [weight_ref[2 * y + x, 0, a:b] for x in range(2) for y, a, b in block_rows(k)], axis=0
        )
        w_back = jnp.concatenate(
            [weight_ref[2 * y + x, 1, a:b] for x in range(2) for y, a, b in block_rows(k)], axis=0
        )
        placing = []
        chosen = []
        for i in range(2):
            match = (token == slots_ref[i, pl.ds(expert, 1), :]).astype(f32).astype(bf16)
            gate = jnp.sum(jnp.where(lane == expert, gates[i], 0.0), axis=1, keepdims=True)
            placing.append(match)
            chosen.append(gate)
            span = pl.ds(SLOTS * i, SLOTS)
            rows_ref[k, span, :] = dot(match, second_ref[i], TN).astype(bf16)
            scaled = (dy_ref[i].astype(f32) * gate).astype(bf16)
            grads_ref[k, span, :] = dot(match, scaled, TN).astype(bf16)
        rows = rows_ref[k]
        grads = grads_ref[k]
        hidden = dot(rows, w_in, NT)
        phi = 0.5 * (1.0 + lax.erf(hidden * (1.0 / math.sqrt(2.0))))
        active = (hidden * phi).astype(bf16)
        slope = phi + hidden * jnp.exp(-0.5 * hidden * hidden) * (1.0 / math.sqrt(2.0 * math.pi))
        active_ref[k] = active
        hidden_grad = (dot(grads, w_back, NT) * slope).astype(bf16)
        hidden_grad_ref[k] = hidden_grad
        produced = dot(active, w_back, NN).astype(bf16)
        rows_grad = dot(hidden_grad, w_in, NN).astype(bf16)
        for i in range(2):
            span = slice(SLOTS * i, SLOTS * (i + 1))
            back_sum[i, :, :D] += dot(placing[i], rows_grad[span], NN)
            output = dot(placing[i], produced[span], NN)
            mix_sum[i] += output * chosen[i]
            gate_grad = jnp.sum(output * dy_ref[i].astype(f32), axis=1, keepdims=True)
            back_sum[i, :, D:] += jnp.where(lane == expert, gate_grad, 0.0)
    for i in range(2):
        back_ref[i, :, :D] = back_sum[i, :, :D].astype(bf16)
        tail = back_sum[i, :, D:]
        high = tail.astype(bf16)
        back_ref[i, :, D : D + LANES] = high
        back_ref[i, :, D + LANES :] = (tail - high.astype(f32)).astype(bf16)
        mix_ref[i] = mix_sum[i].astype(bf16)


def pair_call(experts, second, dy, slots, router, weights):
    vmem = pl.BlockSpec(memory_space=pltpu.VMEM)
    length = 2 * SLOTS
    return pl.pallas_call(
        pair_kernel,
        out_shape=(
            jax.ShapeDtypeStruct((2, TOKENS, D + 2 * LANES), bf16),
            jax.ShapeDtypeStruct((2, TOKENS, D), bf16),
            jax.ShapeDtypeStruct((BLOCKS, length, D), bf16),
            jax.ShapeDtypeStruct((BLOCKS, length, D), bf16),
            jax.ShapeDtypeStruct((BLOCKS, length, WIDE), bf16),
            jax.ShapeDtypeStruct((BLOCKS, length, WIDE), bf16),
        ),
        in_specs=[pl.BlockSpec(memory_space=pltpu.SMEM)] + [vmem] * 5,
        out_specs=(vmem,) * 6,
        scratch_shapes=[
            pltpu.VMEM((2, TOKENS, D + LANES), f32),
            pltpu.VMEM((2, TOKENS, D), f32),
        ],
        compiler_params=pltpu.CompilerParams(vmem_limit_bytes=48 * 1024 * 1024),
        cost_estimate=pl.CostEstimate(
            flops=4_000_000_000, bytes_accessed=9_000_000, transcendentals=700_000
        ),
    )(experts, second, dy, slots, router, weights)


def weight_kernel(*refs):
    rows, grads, active, hidden_grad = (refs[ZS * n : ZS * (n + 1)] for n in range(4))
    out_ref = refs[4 * ZS]
    for k in range(BLOCKS):
        for part, (left, right) in enumerate(((hidden_grad, rows), (active, grads))):
            total = dot(left[0][k], right[0][k], TN)
            for n in range(1, ZS):
                total += dot(left[n][k], right[n][k], TN)
            done = 0
            for x in range(2):
                for y, a, b in block_rows(k):
                    out_ref[2 * y + x, part, a:b] = total[done : done + b - a].astype(bf16)
                    done += b - a


def weight_call(saved):
    vmem = pl.BlockSpec(memory_space=pltpu.VMEM)
    operands = [saved[n][which] for which in range(4) for n in range(ZS)]
    return pl.pallas_call(
        weight_kernel,
        out_shape=jax.ShapeDtypeStruct((4, 2, PIECE_ROWS, D), bf16),
        in_specs=[vmem] * len(operands),
        out_specs=vmem,
        compiler_params=pltpu.CompilerParams(vmem_limit_bytes=48 * 1024 * 1024),
        cost_estimate=pl.CostEstimate(
            flops=4_100_000_000, bytes_accessed=20_000_000, transcendentals=0
        ),
    )(*operands)


def pick(value, index, axis=0):
    return lax.dynamic_index_in_dim(value, index, axis, keepdims=False)


def scatter_rows(place, value):
    columns = value.shape[1]
    m = place.teams
    each = D // (TEAM * m)
    value = value.astype(bf16).reshape(4, 2, m, 2, 2 * each, columns)
    value = value.transpose(0, 1, 3, 2, 4, 5).reshape(4, 2, 2, m * 2 * each, columns)
    cut = (columns // 2 + LANES - 1) // LANES * LANES
    results = []
    for part, order in ((value[..., :cut], "xy"), (value[..., cut:], "yx")):
        for axis in order:
            if axis == "x":
                side, here, moved = 2 if order == "xy" else 1, place.x, (0, 1)
            else:
                side, here, moved = 1, place.y, (1, 0)
            kept = pick(part, here, side).astype(f32)
            got = place.flip(pick(part, 1 - here, side), *moved).astype(f32)
            part = (kept + got).astype(bf16)
        total = pick(part, place.z).astype(f32)
        for k in range(1, ZS):
            total += place.roll(pick(part, (place.z + k) % ZS), k).astype(f32)
        results.append(total)
    total = jnp.concatenate(results, axis=-1).reshape(m, 2 * each, columns)
    if m > 1:
        total = lax.psum_scatter(
            total, "fsdp", scatter_dimension=0, axis_index_groups=place.team_groups()
        )
    return total.reshape(2, each, columns)


def by_core(place, mine, other):
    first = place.core == 0
    return jnp.stack([jnp.where(first, mine, other), jnp.where(first, other, mine)], axis=-2)


def local(images, slots, small_params, qkv_weight, out_weight, expert_in, expert_out, cotangent):
    place = Place()
    teams = place.teams
    each = D // (TEAM * teams)
    core = place.core
    layer = jnp.concatenate(
        [
            qkv_weight.reshape(each, 3 * D),
            out_weight.reshape(each, D),
            jnp.pad(small_params.reshape(each, 8), ((0, 0), (0, LANES - 8))),
        ],
        axis=1,
    )
    layer = lax.all_gather(layer, "fsdp", axis=0, tiled=True)
    piece_in, piece_back = expert_in.reshape(-1, D), expert_out.reshape(-1, D)
    if teams > 1:
        piece_in, piece_back = (
            lax.all_gather(
                piece, "fsdp", axis=0, tiled=True, axis_index_groups=place.team_groups()
            )
            for piece in (piece_in, piece_back)
        )
    turned = turn(place, piece_in)
    weights = lax.all_gather(
        jnp.stack([turned, piece_back]), "fsdp", axis=0, axis_index_groups=place.plane_groups()
    )

    image = images[0]
    inputs = image.astype(f32)
    pair = jnp.stack([image, place.swap_core(image)]).astype(f32)
    codes = jnp.pad(
        jnp.where(slots[0] >= 0, slots[0] // 2, -1),
        ((0, 8 - EXPERTS), (0, SLOTS - CAP)),
        constant_values=-1,
    )
    dy_own = jnp.pad(cotangent[0], ((0, TOKENS - PATCHES), (0, 0)))

    def to_pairs(value):
        moved = [value] + [place.roll(value, k) for k in range(1, ZS)]
        return [jnp.stack([v, place.swap_core(v)]) for v in moved]

    code_pairs = to_pairs(codes)
    dy_pairs = to_pairs(dy_own)

    small = layer[:, 4 * D : 4 * D + 8].reshape(-1)
    gain_one, bias_one, gain_two, bias_two, bias_out = (
        small[n * D : (n + 1) * D].astype(f32) for n in range(5)
    )
    router = jnp.pad(small[5 * D :].reshape(D, EXPERTS), ((0, 0), (0, LANES - EXPERTS)))
    w_out = layer[:, 3 * D : 4 * D]
    w_qkv = jnp.concatenate(
        [lax.dynamic_slice(layer, (0, n * D + HALF * core), (D, HALF)) for n in range(3)], axis=1
    )

    score_scale = 1.0 / math.sqrt(HEAD_DIM)
    first_value, unit_one, inverse_one = norm_forward(pair, gain_one, bias_one)
    first = first_value.astype(bf16)
    packed = jnp.einsum("gsd,de->gse", first, w_qkv, preferred_element_type=f32).astype(bf16)
    heads = packed.reshape(2, PATCHES, 3, HEADS // 2, HEAD_DIM)
    queries, keys, values = heads[:, :, 0], heads[:, :, 1], heads[:, :, 2]
    scores = jnp.einsum("gqhe,gkhe->ghqk", queries, keys, preferred_element_type=f32) * score_scale
    peak = jnp.max(scores, axis=-1, keepdims=True)
    powers = jnp.exp(scores - peak)
    exact = powers / jnp.sum(powers, axis=-1, keepdims=True)
    probabilities = exact.astype(bf16)
    attended_part = (
        jnp.einsum("ghqk,gkhe->gqhe", probabilities, values, preferred_element_type=f32)
        .reshape(2, PATCHES, HALF)
        .astype(bf16)
    )
    attended = by_core(place, attended_part[0], place.swap_core(attended_part[1]))
    attended = attended.reshape(PATCHES, D)
    middle = inputs + dot(attended, w_out, NN) + bias_out
    second_value, unit_two, inverse_two = norm_forward(middle, gain_two, bias_two)
    second = second_value.astype(bf16)

    experts = (BLOCKS * place.z + jnp.arange(BLOCKS, dtype=jnp.int32)) // ZS
    second_pairs = to_pairs(jnp.pad(second, ((0, TOKENS - PATCHES), (0, 0))))
    results = [
        pair_call(experts, second_pairs[k], dy_pairs[k], code_pairs[k], router, weights)
        for k in range(ZS)
    ]

    def collect(which):
        total = 0
        for k in range(ZS):
            part = results[k][which]
            part = part[0].astype(f32) + place.swap_core(part[1]).astype(f32)
            if k:
                part = place.roll(part.astype(bf16), -k).astype(f32)
            total = total + part
        return total[:PATCHES]

    back = collect(0)
    expert_grads = weight_call([result[2:] for result in results])
    block_output = (middle + collect(1)).astype(bf16)

    here = 2 * place.y + place.x
    summed = pick(expert_grads, here).astype(f32)
    for dy, dx in ((0, 1), (1, 0), (1, 1)):
        summed += place.flip(pick(expert_grads, here ^ (2 * dy + dx)), dy, dx).astype(f32)
    in_grad, back_grad = turn(place, summed[0].astype(bf16)).astype(f32), summed[1]
    if teams > 1:
        in_grad, back_grad = (
            lax.psum_scatter(
                grad,
                "fsdp",
                scatter_dimension=0,
                tiled=True,
                axis_index_groups=place.team_groups(),
            )
            for grad in (in_grad, back_grad)
        )

    token_of = codes[:EXPERTS, :CAP]
    there = jnp.any(
        token_of[None] == jnp.arange(PATCHES, dtype=jnp.int32)[:, None, None], axis=-1
    )
    logits = dot(second, router, NN)[:, :EXPERTS]
    gates = jax.nn.softmax(jnp.where(there, logits, -jnp.inf), axis=-1)
    gate_grad = back[:, D : D + EXPERTS] + back[:, D + LANES : D + LANES + EXPERTS]
    logit_grad = gates * (gate_grad - jnp.sum(gates * gate_grad, axis=-1, keepdims=True))
    logit_grad = jnp.where(there, logit_grad, 0.0).astype(bf16)
    second_grad = back[:, :D] + dot(logit_grad, router[:, :EXPERTS], NT)
    router_grad = dot(second, logit_grad, TN)
    middle_back, gain_two_grad, bias_two_grad = norm_backward(
        second_grad, unit_two, inverse_two, gain_two
    )
    middle_grad = cotangent[0].astype(f32) + middle_back
    bias_out_grad = jnp.sum(middle_grad, axis=0)
    proj_grad = middle_grad.astype(bf16)
    attended_grad = dot(proj_grad, w_out, NT).astype(bf16)
    halves = attended_grad.reshape(PATCHES, 2, HALF)
    attended_grad = jnp.stack(
        [pick(halves, core, 1), place.swap_core(pick(halves, 1 - core, 1))]
    ).reshape(2, PATCHES, HEADS // 2, HEAD_DIM)
    proj_weight_grad = dot(attended, proj_grad, TN).reshape(D, 2, HALF)
    proj_weight_grad = pick(proj_weight_grad, core, 1) + place.swap_core(
        pick(proj_weight_grad, 1 - core, 1).astype(bf16)
    ).astype(f32)
    out_rows = scatter_rows(place, proj_weight_grad)

    prob_grad = jnp.einsum("gqhe,gkhe->ghqk", attended_grad, values, preferred_element_type=f32)
    score_grad = (
        exact * (prob_grad - jnp.sum(exact * prob_grad, axis=-1, keepdims=True))
    ).astype(bf16)
    query_grad = (
        jnp.einsum("ghqk,gkhe->gqhe", score_grad, keys, preferred_element_type=f32) * score_scale
    )
    key_grad = (
        jnp.einsum("ghqk,gqhe->gkhe", score_grad, queries, preferred_element_type=f32)
        * score_scale
    )
    value_grad = jnp.einsum(
        "ghqk,gqhe->gkhe", probabilities, attended_grad, preferred_element_type=f32
    )
    qkv_grad = jnp.concatenate(
        [grad.reshape(2, PATCHES, HALF) for grad in (query_grad, key_grad, value_grad)], axis=-1
    ).astype(bf16)
    first_grad = jnp.einsum("gse,de->gsd", qkv_grad, w_qkv, preferred_element_type=f32)
    first_grad = first_grad[0] + place.swap_core(first_grad[1].astype(bf16)).astype(f32)
    packed_weight_grad = jnp.einsum("gsd,gse->de", first, qkv_grad, preferred_element_type=f32)
    input_back, gain_one_grad, bias_one_grad = norm_backward(
        first_grad, unit_one[0], inverse_one[0], gain_one
    )
    input_grad = (middle_grad + input_back).astype(bf16)
    small_terms = jnp.concatenate(
        [
            gain_one_grad,
            bias_one_grad,
            gain_two_grad,
            bias_two_grad,
            bias_out_grad,
            router_grad.reshape(-1),
        ]
    ).reshape(D, 2, 4)
    small_terms = pick(small_terms, core, 1) + place.swap_core(pick(small_terms, 1 - core, 1))
    small_terms = jnp.pad(small_terms, ((0, 0), (0, LANES - 4)))
    late_rows = scatter_rows(place, jnp.concatenate([packed_weight_grad, small_terms], axis=1))
    rows = jnp.concatenate([late_rows, out_rows], axis=-1)
    mine = pick(rows, core)
    other = place.swap_core(pick(rows, 1 - core).astype(bf16)).astype(f32)

    def joined(a, b, count):
        cut = [half[:, a:b].reshape(each, count, -1) for half in (mine, other)]
        return by_core(place, *cut).reshape(-1)

    small_grad = joined(3 * HALF, 3 * HALF + 4, 1)
    qkv_weight_grad = joined(0, 3 * HALF, 3)
    out_weight_grad = joined(3 * HALF + LANES, 4 * HALF + LANES, 1)
    return (
        block_output[None],
        input_grad[None],
        small_grad,
        qkv_weight_grad,
        out_weight_grad,
        in_grad.reshape(-1),
        back_grad.reshape(-1),
    )


def solution(mesh):
    rows = P("fsdp", None, None)
    flat = P("fsdp")
    return jax.shard_map(
        local,
        mesh=mesh,
        in_specs=(rows, rows, flat, flat, flat, flat, flat, rows),
        out_specs=(rows, rows, flat, flat, flat, flat, flat),
        check_vma=False,
    )
```

```python
import functools
import math

import jax
import jax.numpy as jnp
from jax import lax
from jax.experimental import pallas as pl
from jax.experimental.pallas import tpu as pltpu
from jax.sharding import PartitionSpec as P

D = 768
HEADS = 12
HEAD_DIM = 64
EXPERTS = 3
GROUP = 4
PATCHES = 197
CAP = 136
EPSILON = 1e-06

ZS = 4
TEAM = 32
PIECES = TEAM // GROUP
PIECE_ROWS = EXPERTS * D // PIECES
STEP = 96
REACH = 3
BLOCK = 192
BLOCKS = 3
WIDE = GROUP * BLOCK
TOKENS = 208
EXTRA = 200
SLOTS = 144
LANES = 128
HALF = D // 2

f32 = jnp.float32
bf16 = jnp.bfloat16


def norm_forward(value, gain, bias):
    average = jnp.mean(value, axis=-1, keepdims=True)
    centred = value - average
    inverse = lax.rsqrt(jnp.mean(centred * centred, axis=-1, keepdims=True) + EPSILON)
    normed = centred * inverse
    return normed * gain + bias, normed, inverse


def norm_backward(incoming, normed, inverse, gain):
    scaled = incoming * gain
    returned = inverse * (
        scaled
        - jnp.mean(scaled, axis=-1, keepdims=True)
        - normed * jnp.mean(scaled * normed, axis=-1, keepdims=True)
    )
    return returned, jnp.sum(incoming * normed, axis=0), jnp.sum(incoming, axis=0)


def dot(a, b, dims):
    return lax.dot_general(a, b, (dims, ((), ())), preferred_element_type=f32)


NN = ((1,), (0,))
NT = ((1,), (1,))
TN = ((0,), (0,))


class Place:
    def __init__(self):
        self.teams = lax.axis_size("fsdp") // TEAM
        index = lax.axis_index("fsdp")
        self.core = index % 2
        self.x = (index // 2) % 2
        self.piece = index // (GROUP * self.teams)
        self.y = self.piece % 2
        self.z = self.piece // 2

    def index(self, z, y, x, core, team):
        return ((2 * z + y) * self.teams + team) * GROUP + 2 * x + core

    def send(self, value, move):
        pairs = []
        for team in range(self.teams):
            for z in range(ZS):
                for y in range(2):
                    for x in range(2):
                        for core in range(2):
                            to = move(z, y, x, core)
                            if to is not None:
                                pairs.append(
                                    (self.index(z, y, x, core, team), self.index(*to, team))
                                )
        return lax.ppermute(value, "fsdp", pairs)

    def swap_core(self, value):
        return self.send(value, lambda z, y, x, c: (z, y, x, 1 - c))

    def flip(self, value, dy, dx):
        return self.send(value, lambda z, y, x, c: (z, y ^ dy, x ^ dx, c))

    def roll(self, value, k):
        return self.send(value, lambda z, y, x, c: ((z + k) % ZS, y, x, c))

    def shift(self, value, s):
        def move(z, y, x, c):
            to = 2 * z + y + s
            return (to // 2, to % 2, x, c) if 0 <= to < PIECES else None

        return self.send(value, move)

    def line_groups(self):
        return [
            [self.index(z, y, x, c, team) for z in range(ZS)]
            for team in range(self.teams)
            for y in range(2)
            for x in range(2)
            for c in range(2)
        ]

    def team_groups(self):
        return [
            [self.index(z, y, x, c, team) for team in range(self.teams)]
            for z in range(ZS)
            for y in range(2)
            for x in range(2)
            for c in range(2)
        ]


def turn(place, piece):
    return turn_join(place, turn_send(place, piece))


def turn_send(place, piece):
    upright = piece.T
    twice = jnp.concatenate([upright, upright], axis=0)
    parts = []
    for s in range(REACH, -REACH - 1, -1):
        start = (PIECE_ROWS * (place.piece + s + PIECES)) % D
        tile = lax.dynamic_slice(twice, (start, 0), (PIECE_ROWS, PIECE_ROWS))
        parts.append(place.shift(tile, s) if s else tile)
    return parts


def turn_join(place, parts):
    row = jnp.concatenate(parts, axis=1)
    steps = PIECE_ROWS // STEP
    blocks = []
    for j in range(steps):
        expert = (steps * place.piece + j) // (D // STEP)
        start = STEP * ((D // STEP) * expert - steps * (place.piece - REACH))
        blocks.append(lax.dynamic_slice(row, (STEP * j, start), (STEP, D)))
    return jnp.concatenate(blocks, axis=0)


def block_rows(k):
    low, high = BLOCK * k, BLOCK * (k + 1)
    found = []
    for y in range(2):
        a, b = max(low, PIECE_ROWS * y), min(high, PIECE_ROWS * (y + 1))
        if a < b:
            found.append((y, a - PIECE_ROWS * y, b - PIECE_ROWS * y))
    return found


def block_weight(refs, k):
    return jnp.concatenate(
        [ref[y, x, a:b] for ref in refs for x in range(2) for y, a, b in block_rows(k)], axis=0
    )


def head_scores(packed, block, odd):
    lane = lax.broadcasted_iota(jnp.int32, (TOKENS, LANES), 1)
    mine = (lane >= HEAD_DIM) if odd else (lane < HEAD_DIM)
    queries = packed[:, LANES * block : LANES * (block + 1)]
    queries = jnp.where(mine, queries, jnp.zeros_like(queries))
    keys = packed[:, HALF + LANES * block : HALF + LANES * (block + 1)]
    scores = dot(queries, keys, NT) * (1.0 / math.sqrt(HEAD_DIM))
    column = lax.broadcasted_iota(jnp.int32, (TOKENS, TOKENS), 1)
    scores = jnp.where(column < PATCHES, scores, -1e30)
    powers = jnp.exp(scores - jnp.max(scores, axis=1, keepdims=True))
    exact = powers / jnp.sum(powers, axis=1, keepdims=True)
    return exact, mine, queries, keys


def attention_kernel(pair_ref, norm_ref, weight_ref, first_ref, packed_ref, attended_ref):
    for i in range(2):
        value = pair_ref[i].astype(f32)
        first, _, _ = norm_forward(value, norm_ref[0:1], norm_ref[1:2])
        first = first.astype(bf16)
        first_ref[i] = first
        packed = dot(first, weight_ref[...], NN).astype(bf16)
        packed_ref[i] = packed
        for block in range(HALF // LANES):
            values = packed[:, 2 * HALF + LANES * block : 2 * HALF + LANES * (block + 1)]
            outs = []
            for odd in range(2):
                exact, mine, _, _ = head_scores(packed, block, odd)
                outs.append(dot(exact.astype(bf16), values, NN))
            attended_ref[i, :, LANES * block : LANES * (block + 1)] = jnp.where(
                mine, outs[1], outs[0]
            ).astype(bf16)


def attention_call(pair, norms, weight):
    vmem = pl.BlockSpec(memory_space=pltpu.VMEM)
    return pl.pallas_call(
        attention_kernel,
        out_shape=(
            jax.ShapeDtypeStruct((2, TOKENS, D), bf16),
            jax.ShapeDtypeStruct((2, TOKENS, 3 * HALF), bf16),
            jax.ShapeDtypeStruct((2, TOKENS, HALF), bf16),
        ),
        in_specs=[vmem] * 3,
        out_specs=(vmem,) * 3,
        compiler_params=pltpu.CompilerParams(vmem_limit_bytes=48 * 1024 * 1024),
        cost_estimate=pl.CostEstimate(
            flops=1_100_000_000, bytes_accessed=5_000_000, transcendentals=500_000
        ),
    )(pair, norms, weight)


def attention_back_kernel(
    packed_ref,
    own_grad_ref,
    other_grad_ref,
    first_ref,
    weight_ref,
    own_ref,
    other_ref,
    left_ref,
    right_ref,
    qkv_ref,
    total_ref,
):
    scale = 1.0 / math.sqrt(HEAD_DIM)
    for i, upper_ref in ((1, other_grad_ref), (0, own_grad_ref)):
        packed = packed_ref[i]
        for block in range(HALF // LANES):
            span = slice(LANES * block, LANES * (block + 1))
            values = packed[:, 2 * HALF + LANES * block : 2 * HALF + LANES * (block + 1)]
            upper = upper_ref[:, span]
            found = []
            for odd in range(2):
                exact, mine, queries, keys = head_scores(packed, block, odd)
                masked = jnp.where(mine, upper, jnp.zeros_like(upper))
                prob_grad = dot(masked, values, NT)
                mean = jnp.sum(exact * prob_grad, axis=1, keepdims=True)
                score_grad = (exact * (prob_grad - mean)).astype(bf16)
                found.append(
                    (
                        dot(score_grad, keys, NN) * scale,
                        dot(score_grad, queries, TN) * scale,
                        dot(exact.astype(bf16), masked, TN),
                    )
                )
            for n in range(3):
                qkv_ref[:, HALF * n + LANES * block : HALF * n + LANES * (block + 1)] = jnp.where(
                    mine, found[1][n], found[0][n]
                ).astype(bf16)
        grads = qkv_ref[...]
        back = dot(grads, weight_ref[...], NT)
        if i == 1:
            other_ref[...] = back.astype(bf16)
            total_ref[...] = dot(first_ref[i], grads, TN)
        else:
            own_ref[...] = back
    total = total_ref[...] + dot(first_ref[0], grads, TN)
    left_ref[...] = total[:, :D].astype(bf16)
    right_ref[...] = total[:, D:].astype(bf16)


def attention_back_call(after, *operands):
    vmem = pl.BlockSpec(memory_space=pltpu.VMEM)
    return pl.pallas_call(
        follow(attention_back_kernel, len(after), len(operands)),
        out_shape=(
            jax.ShapeDtypeStruct((TOKENS, D), f32),
            jax.ShapeDtypeStruct((TOKENS, D), bf16),
            jax.ShapeDtypeStruct((D, D), bf16),
            jax.ShapeDtypeStruct((D, HALF), bf16),
        ),
        in_specs=[vmem] * len(operands) + [pl.BlockSpec(memory_space=pl.ANY)] * len(after),
        out_specs=(vmem,) * 4,
        scratch_shapes=[
            pltpu.VMEM((TOKENS, 3 * HALF), bf16),
            pltpu.VMEM((D, 3 * HALF), f32),
        ],
        compiler_params=pltpu.CompilerParams(vmem_limit_bytes=48 * 1024 * 1024),
        cost_estimate=pl.CostEstimate(
            flops=2_500_000_000, bytes_accessed=8_000_000, transcendentals=500_000
        ),
    )(*operands, *after)


def find_gates(second, router, codes_ref):
    lane = lax.broadcasted_iota(jnp.int32, (TOKENS, LANES), 1)
    token = lax.broadcasted_iota(jnp.int32, (TOKENS, SLOTS), 0)
    there = jnp.zeros((TOKENS, LANES), f32)
    for e in range(EXPERTS):
        match = (token == codes_ref[e : e + 1, :]).astype(f32)
        there = jnp.where(lane == e, jnp.max(match, axis=1, keepdims=True), there)
    logits = dot(second, router, NN)
    masked = jnp.where(there > 0, logits, -1e30)
    peak = jnp.max(masked, axis=1, keepdims=True)
    weight = jnp.where(there > 0, jnp.exp(masked - peak), 0.0)
    total = jnp.sum(weight, axis=1, keepdims=True)
    return weight / jnp.where(total > 0, total, 1.0)


def middle_kernel(
    core_ref, mine_ref, other_ref, image_ref, own_w, other_w, norm_ref, middle_ref, second_ref
):
    core = core_ref[0]
    here, there = (pl.multiple_of(HALF * c, LANES) for c in (core, 1 - core))
    for columns, w in ((here, own_w), (there, other_w)):
        middle_ref[:, pl.ds(columns, HALF)] = dot(
            mine_ref[...], w[pl.ds(here, HALF), :], NN
        ) + dot(other_ref[...], w[pl.ds(there, HALF), :], NN)
    middle = image_ref[...].astype(f32) + middle_ref[...] + norm_ref[2:3]
    middle_ref[...] = middle
    second, _, _ = norm_forward(middle, norm_ref[0:1], norm_ref[1:2])
    second_ref[...] = second.astype(bf16)


def middle_call(core, mine, other, image, own_w, other_w, norms):
    vmem = pl.BlockSpec(memory_space=pltpu.VMEM)
    return pl.pallas_call(
        middle_kernel,
        out_shape=(
            jax.ShapeDtypeStruct((TOKENS, D), f32),
            jax.ShapeDtypeStruct((TOKENS, D), bf16),
        ),
        in_specs=[pl.BlockSpec(memory_space=pltpu.SMEM)] + [vmem] * 6,
        out_specs=(vmem,) * 2,
        compiler_params=pltpu.CompilerParams(vmem_limit_bytes=32 * 1024 * 1024),
        cost_estimate=pl.CostEstimate(
            flops=250_000_000, bytes_accessed=3_500_000, transcendentals=0
        ),
    )(core, mine, other, image, own_w, other_w, norms)


def middle_back_kernel(
    core_ref,
    back0_ref,
    back1_ref,
    back2_ref,
    back3_ref,
    second_ref,
    middle_ref,
    dy_ref,
    router_ref,
    own_w,
    other_w,
    norm_ref,
    mine_ref,
    other_ref,
    grad_ref,
    mine_grad_ref,
    other_grad_ref,
    own_cols_ref,
    other_cols_ref,
    vector_ref,
    router_grad_ref,
    total_ref,
    spare_ref,
    codes_ref,
    proj_ref,
):
    core = core_ref[0]
    here, there = (pl.multiple_of(HALF * c, LANES) for c in (core, 1 - core))
    total_ref[...] = (
        back0_ref[...].astype(f32)
        + back1_ref[...].astype(f32)
        + back2_ref[...].astype(f32)
        + back3_ref[...].astype(f32)
    )
    codes_ref[...] = dy_ref[EXTRA:, :SLOTS].astype(f32).astype(jnp.int32)
    lane = lax.broadcasted_iota(jnp.int32, (TOKENS, LANES), 1)
    real = lax.broadcasted_iota(jnp.int32, (TOKENS, D), 0) < PATCHES
    second = second_ref[...]
    gates = find_gates(second, router_ref[...], codes_ref)
    spare_ref[...] = jnp.zeros_like(spare_ref)
    spare = total_ref[EXTRA:, : 2 * LANES]
    spare_ref[:8] = spare + pltpu.roll(spare, 4, 0)
    gate_grad = jnp.where(lane < EXPERTS, spare_ref[...].T[:TOKENS], 0.0)
    mean = jnp.sum(gates * gate_grad, axis=1, keepdims=True)
    logit_grad = (gates * (gate_grad - mean)).astype(bf16)
    second_grad = total_ref[...] + dot(logit_grad, router_ref[...], NT)
    second_grad = jnp.where(real, second_grad, 0.0)
    router_grad_ref[...] = dot(second, logit_grad, TN)
    _, unit, inverse = norm_forward(middle_ref[...], norm_ref[0:1], norm_ref[1:2])
    back, gain_grad, bias_grad = norm_backward(second_grad, unit, inverse, norm_ref[0:1])
    middle_grad = jnp.where(real, dy_ref[...].astype(f32) + back, 0.0)
    grad_ref[...] = middle_grad
    vector_ref[...] = jnp.zeros_like(vector_ref)
    vector_ref[0:1] = gain_grad[None]
    vector_ref[1:2] = bias_grad[None]
    vector_ref[2:3] = jnp.sum(middle_grad, axis=0)[None]
    proj_ref[...] = middle_grad.astype(bf16)
    own = proj_ref[:, pl.ds(here, HALF)]
    other = proj_ref[:, pl.ds(there, HALF)]
    for rows, out_ref in ((here, mine_grad_ref), (there, other_grad_ref)):
        out_ref[...] = (
            dot(own, own_w[pl.ds(rows, HALF), :], NT) + dot(other, other_w[pl.ds(rows, HALF), :], NT)
        ).astype(bf16)
    for columns, out_ref in ((own, own_cols_ref), (other, other_cols_ref)):
        out_ref[pl.ds(here, HALF), :] = dot(mine_ref[...], columns, TN).astype(bf16)
        out_ref[pl.ds(there, HALF), :] = dot(other_ref[...], columns, TN).astype(bf16)


def middle_back_call(after, core, *operands):
    vmem = pl.BlockSpec(memory_space=pltpu.VMEM)
    return pl.pallas_call(
        follow(middle_back_kernel, len(after), 1 + len(operands)),
        out_shape=(
            jax.ShapeDtypeStruct((TOKENS, D), f32),
            jax.ShapeDtypeStruct((TOKENS, HALF), bf16),
            jax.ShapeDtypeStruct((TOKENS, HALF), bf16),
            jax.ShapeDtypeStruct((D, HALF), bf16),
            jax.ShapeDtypeStruct((D, HALF), bf16),
            jax.ShapeDtypeStruct((8, D), f32),
            jax.ShapeDtypeStruct((D, LANES), f32),
        ),
        in_specs=[pl.BlockSpec(memory_space=pltpu.SMEM)]
        + [vmem] * len(operands)
        + [pl.BlockSpec(memory_space=pl.ANY)] * len(after),
        out_specs=(vmem,) * 7,
        scratch_shapes=[
            pltpu.VMEM((TOKENS, D), f32),
            pltpu.VMEM((LANES, 2 * LANES), f32),
            pltpu.VMEM((TOKENS - EXTRA, SLOTS), jnp.int32),
            pltpu.VMEM((TOKENS, D), bf16),
        ],
        compiler_params=pltpu.CompilerParams(vmem_limit_bytes=48 * 1024 * 1024),
        cost_estimate=pl.CostEstimate(
            flops=800_000_000, bytes_accessed=8_000_000, transcendentals=0
        ),
    )(core, *operands, *after)


def follow(kernel, count, n_in):
    def wrapped(*refs):
        return kernel(*refs[:n_in], *refs[n_in + count :])

    return wrapped


def last_kernel(own_ref, arrived_ref, image_ref, norm_ref, middle_grad_ref, grad_ref, vector_ref):
    incoming = own_ref[...] + arrived_ref[...].astype(f32)
    real = lax.broadcasted_iota(jnp.int32, (TOKENS, D), 0) < PATCHES
    incoming = jnp.where(real, incoming, 0.0)
    _, unit, inverse = norm_forward(image_ref[...].astype(f32), norm_ref[0:1], norm_ref[1:2])
    back, gain_grad, bias_grad = norm_backward(incoming, unit, inverse, norm_ref[0:1])
    grad_ref[...] = (middle_grad_ref[...] + back).astype(bf16)
    vector_ref[...] = jnp.zeros_like(vector_ref)
    vector_ref[0:1] = gain_grad[None]
    vector_ref[1:2] = bias_grad[None]


def last_call(after, *operands):
    vmem = pl.BlockSpec(memory_space=pltpu.VMEM)
    return pl.pallas_call(
        follow(last_kernel, len(after), len(operands)),
        out_shape=(
            jax.ShapeDtypeStruct((TOKENS, D), bf16),
            jax.ShapeDtypeStruct((8, D), f32),
        ),
        in_specs=[vmem] * len(operands) + [pl.BlockSpec(memory_space=pl.ANY)] * len(after),
        out_specs=(vmem,) * 2,
        compiler_params=pltpu.CompilerParams(vmem_limit_bytes=24 * 1024 * 1024),
        cost_estimate=pl.CostEstimate(flops=2_000_000, bytes_accessed=2_500_000, transcendentals=0),
    )(*operands, *after)


def image_kernel(
    expert_ref,
    second_ref,
    dy_ref,
    router_ref,
    own_in_ref,
    other_in_ref,
    own_back_ref,
    other_back_ref,
    back_ref,
    mix_ref,
    rows_ref,
    grads_ref,
    active_ref,
    hidden_grad_ref,
    back_sum,
    gate_sum,
    mix_sum,
    codes_ref,
):
    lane = lax.broadcasted_iota(jnp.int32, (TOKENS, LANES), 1)
    token = lax.broadcasted_iota(jnp.int32, (TOKENS, SLOTS), 0)
    codes_ref[...] = dy_ref[EXTRA:, :SLOTS].astype(f32).astype(jnp.int32)
    gates = find_gates(second_ref[...], router_ref[...], codes_ref)
    gate_sum[...] = jnp.zeros_like(gate_sum)
    for k in range(BLOCKS):
        expert = expert_ref[k]
        w_in = block_weight((own_in_ref, other_in_ref), k)
        w_back = block_weight((own_back_ref, other_back_ref), k)
        placing = (token == codes_ref[pl.ds(expert, 1), :]).astype(f32).astype(bf16)
        gate = jnp.sum(jnp.where(lane == expert, gates, 0.0), axis=1, keepdims=True)
        rows = dot(placing, second_ref[...], TN).astype(bf16)
        scaled = (dy_ref[...].astype(f32) * gate).astype(bf16)
        grads = dot(placing, scaled, TN).astype(bf16)
        rows_ref[k] = rows
        grads_ref[k] = grads
        hidden = dot(rows, w_in, NT)
        phi = 0.5 * (1.0 + lax.erf(hidden * (1.0 / math.sqrt(2.0))))
        active = (hidden * phi).astype(bf16)
        slope = phi + hidden * jnp.exp(-0.5 * hidden * hidden) * (1.0 / math.sqrt(2.0 * math.pi))
        active_ref[k] = active
        hidden_grad = (dot(grads, w_back, NT) * slope).astype(bf16)
        hidden_grad_ref[k] = hidden_grad
        produced = dot(active, w_back, NN).astype(bf16)
        rows_grad = dot(hidden_grad, w_in, NN).astype(bf16)
        output = dot(placing, produced, NN)
        gate_grad = jnp.sum(output * dy_ref[...].astype(f32), axis=1, keepdims=True)
        gate_sum[:TOKENS] += jnp.where(lane == expert, gate_grad, 0.0)
        if k == 0:
            back_sum[...] = dot(placing, rows_grad, NN)
            mix_sum[...] = output * gate
        else:
            back_sum[...] += dot(placing, rows_grad, NN)
            mix_sum[...] += output * gate
    spare = gate_sum[...].T[:8]
    high = spare.astype(bf16).astype(f32)
    low = (spare - high).astype(bf16).astype(f32)
    row = lax.broadcasted_iota(jnp.int32, spare.shape, 0)
    back_sum[EXTRA:, : 2 * LANES] = jnp.where(row < 4, high, pltpu.roll(low, 4, 0))
    back_ref[...] = back_sum[...].astype(bf16)
    mix_ref[...] = mix_sum[...].astype(bf16)


def image_call(after, experts, second, dy, router, *weights):
    vmem = pl.BlockSpec(memory_space=pltpu.VMEM)
    return pl.pallas_call(
        follow(image_kernel, len(after), 8),
        out_shape=(
            jax.ShapeDtypeStruct((TOKENS, D), bf16),
            jax.ShapeDtypeStruct((TOKENS, D), bf16),
            jax.ShapeDtypeStruct((BLOCKS, SLOTS, D), bf16),
            jax.ShapeDtypeStruct((BLOCKS, SLOTS, D), bf16),
            jax.ShapeDtypeStruct((BLOCKS, SLOTS, WIDE), bf16),
            jax.ShapeDtypeStruct((BLOCKS, SLOTS, WIDE), bf16),
        ),
        in_specs=[pl.BlockSpec(memory_space=pltpu.SMEM)]
        + [vmem] * 7
        + [pl.BlockSpec(memory_space=pl.ANY)] * len(after),
        out_specs=(vmem,) * 6,
        scratch_shapes=[
            pltpu.VMEM((TOKENS, D), f32),
            pltpu.VMEM((2 * LANES, LANES), f32),
            pltpu.VMEM((TOKENS, D), f32),
            pltpu.VMEM((TOKENS - EXTRA, SLOTS), jnp.int32),
        ],
        compiler_params=pltpu.CompilerParams(vmem_limit_bytes=48 * 1024 * 1024),
        cost_estimate=pl.CostEstimate(
            flops=1, bytes_accessed=1, transcendentals=0
        ),
    )(experts, second, dy, router, *weights, *after)


def weight_kernel(*refs):
    lefts, rights, outs = refs[:ZS], refs[ZS : 2 * ZS], refs[2 * ZS :]
    for half, out_ref in zip((1, 0), outs):
        span = slice(half * WIDE // 2, (half + 1) * WIDE // 2)
        for k in range(BLOCKS):
            total = dot(lefts[0][k, :, span], rights[0][k], TN)
            for n in range(1, ZS):
                total += dot(lefts[n][k, :, span], rights[n][k], TN)
            done = 0
            for x in range(2):
                for y, a, b in block_rows(k):
                    out_ref[y, x, a:b] = total[done : done + b - a].astype(bf16)
                    done += b - a


def weight_call(after, *operands):
    vmem = pl.BlockSpec(memory_space=pltpu.VMEM)
    return pl.pallas_call(
        follow(weight_kernel, len(after), len(operands)),
        out_shape=(jax.ShapeDtypeStruct((2, 2, PIECE_ROWS, D), bf16),) * 2,
        in_specs=[vmem] * len(operands) + [pl.BlockSpec(memory_space=pl.ANY)] * len(after),
        out_specs=(vmem,) * 2,
        compiler_params=pltpu.CompilerParams(vmem_limit_bytes=48 * 1024 * 1024),
        cost_estimate=pl.CostEstimate(
            flops=4_100_000_000, bytes_accessed=9_000_000, transcendentals=0
        ),
    )(*operands, *after)


def pick(value, index, axis=0):
    return lax.dynamic_index_in_dim(value, index, axis, keepdims=False)


def add_rows(kept, got):
    return (kept.astype(f32) + got.astype(f32)).astype(bf16)


def scatter_parts(place, value):
    m = place.teams
    value = value.reshape(4, 2, m, 2, 2 * D // (TEAM * m), -1)
    return value.transpose(0, 1, 3, 2, 4, 5).reshape(4, 2, 2, 2 * D // TEAM, -1)


def scatter_rows(place, left, right, held):
    m = place.teams
    each = D // (TEAM * m)

    def fold(part, axis, side):
        here, move = (place.x, (0, 1)) if axis == "x" else (place.y, (1, 0))
        return add_rows(pick(part, here, side), place.flip(pick(part, 1 - here, side), *move))

    right = fold(scatter_parts(place, right), "y", 1)
    left, right, held = lax.optimization_barrier((left, right, held))
    left, right = fold(left, "y", 1), fold(right, "x", 1)
    both = jnp.concatenate([left, right], axis=-1)
    total = pick(both, place.z).astype(f32)
    for k in range(1, ZS):
        total += place.roll(pick(both, (place.z + k) % ZS), k).astype(f32)
    total = total.reshape(m, 2 * each, -1)
    if m > 1:
        total = lax.psum_scatter(
            total, "fsdp", scatter_dimension=0, axis_index_groups=place.team_groups()
        )
    return total.reshape(2, each, -1), held


def in_order(index, mine, other, axis):
    first = index == 0
    return jnp.stack([jnp.where(first, mine, other), jnp.where(first, other, mine)], axis=axis)


def by_core(place, mine, other):
    first = place.core == 0
    return jnp.stack([jnp.where(first, mine, other), jnp.where(first, other, mine)], axis=-2)


def local(images, slots, small_params, qkv_weight, out_weight, expert_in, expert_out, cotangent):
    place = Place()
    teams = place.teams
    each = D // (TEAM * teams)
    core = place.core
    qkv_rows = qkv_weight.reshape(each, 3, 2, HALF)
    out_rows = out_weight.reshape(each, 2, HALF)
    small_rows = jnp.pad(small_params.reshape(each, 8), ((0, 0), (0, LANES - 8)))

    def half_rows(c):
        return jnp.concatenate(
            [pick(qkv_rows, c, 2).reshape(each, 3 * HALF), small_rows, pick(out_rows, c, 1)], axis=1
        )

    layer = in_order(core, half_rows(core), place.swap_core(half_rows(1 - core)), 0)
    layer = lax.all_gather(
        layer.reshape(2 * each, -1),
        "fsdp",
        axis=0,
        tiled=True,
        axis_index_groups=[list(range(c, teams * TEAM, 2)) for c in range(2)],
    )
    piece_in, piece_back = expert_in.reshape(-1, D), expert_out.reshape(-1, D)
    if teams > 1:
        piece_in, piece_back = (
            lax.all_gather(
                piece, "fsdp", axis=0, tiled=True, axis_index_groups=place.team_groups()
            )
            for piece in (piece_in, piece_back)
        )

    codes = jnp.where(slots[0] >= 0, slots[0] // 2, -1)
    dy_own = jnp.pad(cotangent[0], ((0, EXTRA - PATCHES), (0, 0)))
    spare = jnp.pad(
        codes, ((0, TOKENS - EXTRA - EXPERTS), (0, D - CAP)), constant_values=-1
    ).astype(bf16)
    dy_own = jnp.concatenate([dy_own, spare], axis=0)

    in_parts = turn_send(place, piece_in)
    dy_own, in_parts = lax.optimization_barrier((dy_own, in_parts))
    dy_moved = {k: place.roll(dy_own, k) if k else dy_own for k in (0, 1, 3, 2)}
    turned = turn_join(place, in_parts)
    moves = ((0, 0), (0, 1), (1, 0), (1, 1))
    weights = ()
    for piece in (turned, piece_back):
        pieces = [place.flip(piece, *move) if any(move) else piece for move in moves]
        if piece is turned:
            pieces, dy_moved = lax.optimization_barrier((pieces, dy_moved))
        own = in_order(place.y, jnp.stack(pieces[:2]), jnp.stack(pieces[2:]), 0)
        weights += (own, place.swap_core(own))

    image = images[0]
    inputs = image.astype(f32)
    pair = jnp.stack([image, place.swap_core(image)])
    pair = jnp.pad(pair, ((0, 0), (0, TOKENS - PATCHES), (0, 0)))
    w_qkv = layer[:, : 3 * HALF]
    small = layer[:, 3 * HALF : 3 * HALF + 8].reshape(-1)
    out_own = layer[:, 3 * HALF + LANES :]
    out_other = place.swap_core(out_own)

    gain_one, bias_one, gain_two, bias_two, bias_out = (
        small[n * D : (n + 1) * D].astype(f32) for n in range(5)
    )
    router = jnp.pad(small[5 * D :].reshape(D, EXPERTS), ((0, 0), (0, LANES - EXPERTS)))
    norms = jnp.stack([gain_one, bias_one])
    first, packed, attended_part = attention_call(pair, norms, w_qkv)
    attended_other = place.swap_core(attended_part[1])
    core_index = core[None].astype(jnp.int32)
    norms_two = jnp.stack([gain_two, bias_two, bias_out])
    middle, second_own = middle_call(
        core_index, attended_part[0], attended_other, pair[0], out_own, out_other, norms_two
    )

    experts = (BLOCKS * place.z + jnp.arange(BLOCKS, dtype=jnp.int32)) // ZS
    moved = {k: place.roll(second_own, k) for k in (1, 3, 2)}
    moved[0] = second_own
    results = {}
    returned = {}
    for k in (0, 1, 3, 2):
        after = [returned[n] for n in list(returned)[:-1][-1:] if n]
        if results:
            after.append(before)
        results[k] = image_call(after, experts, moved[k], dy_moved[k], router, *weights)
        before = results[k][0]
        returned[k] = place.roll(before, -k) if k else before
    rows, grads, active, hidden_grad = zip(*(result[2:] for result in results.values()))

    def chip_sum(other, own):
        return (own.astype(f32) + place.swap_core(other).astype(f32)).astype(bf16)

    def spread(chip):
        here, there = pick(chip, place.y), pick(chip, 1 - place.y)
        return [
            here[0],
            place.flip(here[1], 0, 1),
            place.flip(there[0], 1, 0),
            place.flip(there[1], 1, 1),
        ]

    in_other, in_own = weight_call([], *hidden_grad, *rows)
    back_other, back_own = weight_call([in_own, returned[2]], *active, *grads)
    in_chip = chip_sum(in_other, in_own)
    in_moved = spread(in_chip)
    back_chip = chip_sum(back_other, back_own)
    back_moved = spread(back_chip)
    (
        middle_grad,
        mine_grad,
        other_grad,
        proj_own,
        proj_other,
        vectors,
        router_grad,
    ) = middle_back_call(
        [in_chip, back_chip],
        core_index,
        *returned.values(),
        second_own,
        middle,
        dy_own,
        router,
        out_own,
        out_other,
        norms_two,
        attended_part[0],
        attended_other,
    )
    arrived_grad = place.swap_core(other_grad)
    mixed = [results[k][1] for k in range(ZS - 1, -1, -1)]
    mixed = lax.dynamic_slice_in_dim(jnp.stack(mixed + mixed), ZS - 1 - place.z, ZS, 0)
    mixed, vectors = lax.optimization_barrier((mixed, vectors))
    mixture = lax.psum_scatter(
        mixed, "fsdp", scatter_dimension=0, axis_index_groups=place.line_groups()
    )

    proj_arrived = place.swap_core(proj_other)

    in_parts = turn_send(place, sum(part.astype(f32) for part in in_moved).astype(bf16))
    first_grad, other_grad, qk_grad, v_grad = attention_back_call(
        in_moved[1:] + back_moved[1:], packed, mine_grad, arrived_grad, first, w_qkv
    )
    qk_parts = scatter_parts(place, qk_grad)
    sent, in_parts = lax.optimization_barrier((pick(qk_parts, 1 - place.x, 2), in_parts))
    qk_got = place.flip(sent, 0, 1)
    input_grad, vectors_one = last_call(
        [], first_grad, place.swap_core(other_grad), pair[0], norms, middle_grad
    )
    input_grad = input_grad[:PATCHES]
    small_terms = jnp.concatenate(
        [
            vectors_one[:2].reshape(-1),
            vectors[:3].reshape(-1),
            router_grad[:, :EXPERTS].reshape(-1),
        ]
    )
    small_terms = small_terms.astype(bf16).reshape(TEAM * teams, -1)
    length = -(-small_terms.shape[1] // LANES)
    small_terms = jnp.pad(
        small_terms, ((0, 0), (0, length * LANES - small_terms.shape[1]))
    ).reshape(TEAM * teams, length, LANES)
    small_terms = jnp.pad(small_terms, ((0, 0), (0, each - length), (0, 0))).reshape(D, LANES)
    proj_grad = (proj_own.astype(f32) + proj_arrived.astype(f32)).astype(bf16)
    rows, back_moved = scatter_rows(
        place,
        add_rows(pick(qk_parts, place.x, 2), qk_got),
        jnp.concatenate([v_grad, proj_grad, small_terms], axis=1),
        back_moved,
    )
    mine = pick(rows, core)
    other = place.swap_core(pick(rows, 1 - core).astype(bf16)).astype(f32)

    def joined(a, b, count):
        cut = [half[:, a:b].reshape(each, count, -1) for half in (mine, other)]
        return by_core(place, *cut).reshape(-1)

    small_grad = mine[:length, 4 * HALF :] + other[:length, 4 * HALF :]
    small_grad = small_grad.reshape(-1)[: 8 * each]
    qkv_weight_grad = joined(0, 3 * HALF, 3)
    out_weight_grad = joined(3 * HALF, 4 * HALF, 1)
    block_output = (middle + mixture.astype(f32))[:PATCHES].astype(bf16)
    in_grad = turn_join(place, in_parts).astype(f32)
    back_grad = sum(part.astype(f32) for part in back_moved)
    if teams > 1:
        in_grad, back_grad = (
            lax.psum_scatter(
                grad,
                "fsdp",
                scatter_dimension=0,
                tiled=True,
                axis_index_groups=place.team_groups(),
            )
            for grad in (in_grad, back_grad)
        )
    return (
        block_output[None],
        input_grad[None],
        small_grad,
        qkv_weight_grad,
        out_weight_grad,
        in_grad.reshape(-1),
        back_grad.reshape(-1),
    )


def solution(mesh):
    rows = P("fsdp", None, None)
    flat = P("fsdp")
    return jax.shard_map(
        local,
        mesh=mesh,
        in_specs=(rows, rows, flat, flat, flat, flat, flat, rows),
        out_specs=(rows, rows, flat, flat, flat, flat, flat),
        check_vma=False,
    )
```

```python
import functools
import math

import jax
import jax.numpy as jnp
from jax import lax
from jax.experimental import pallas as pl
from jax.experimental.pallas import tpu as pltpu
from jax.sharding import PartitionSpec as P

D = 768
HEADS = 12
HEAD_DIM = 64
EXPERTS = 3
GROUP = 4
PATCHES = 197
CAP = 136
EPSILON = 1e-06

ZS = 4
TEAM = 32
PIECES = TEAM // GROUP
PIECE_ROWS = EXPERTS * D // PIECES
STEP = 96
REACH = 3
BLOCK = 192
BLOCKS = 3
WIDE = GROUP * BLOCK
TOKENS = 208
EXTRA = 200
SLOTS = 144
LANES = 128
HALF = D // 2

f32 = jnp.float32
bf16 = jnp.bfloat16


def norm_forward(value, gain, bias):
    average = jnp.mean(value, axis=-1, keepdims=True)
    centred = value - average
    inverse = lax.rsqrt(jnp.mean(centred * centred, axis=-1, keepdims=True) + EPSILON)
    normed = centred * inverse
    return normed * gain + bias, normed, inverse


def norm_backward(incoming, normed, inverse, gain):
    scaled = incoming * gain
    returned = inverse * (
        scaled
        - jnp.mean(scaled, axis=-1, keepdims=True)
        - normed * jnp.mean(scaled * normed, axis=-1, keepdims=True)
    )
    return returned, jnp.sum(incoming * normed, axis=0), jnp.sum(incoming, axis=0)


def dot(a, b, dims):
    return lax.dot_general(a, b, (dims, ((), ())), preferred_element_type=f32)


NN = ((1,), (0,))
NT = ((1,), (1,))
TN = ((0,), (0,))


def experts_of(piece):
    steps = PIECE_ROWS // STEP
    return {(steps * piece + j) // (D // STEP) for j in range(steps)}


class Place:
    def __init__(self):
        self.teams = lax.axis_size("fsdp") // TEAM
        index = lax.axis_index("fsdp")
        self.core = index % 2
        self.x = (index // 2) % 2
        self.piece = index // (GROUP * self.teams)
        self.y = self.piece % 2
        self.z = self.piece // 2

    def index(self, z, y, x, core, team):
        return ((2 * z + y) * self.teams + team) * GROUP + 2 * x + core

    def send(self, value, move):
        pairs = []
        for team in range(self.teams):
            for z in range(ZS):
                for y in range(2):
                    for x in range(2):
                        for core in range(2):
                            to = move(z, y, x, core)
                            if to is not None:
                                pairs.append(
                                    (self.index(z, y, x, core, team), self.index(*to, team))
                                )
        return lax.ppermute(value, "fsdp", pairs)

    def swap_core(self, value):
        return self.send(value, lambda z, y, x, c: (z, y, x, 1 - c))

    def flip(self, value, dy, dx):
        return self.send(value, lambda z, y, x, c: (z, y ^ dy, x ^ dx, c))

    def roll(self, value, k):
        return self.send(value, lambda z, y, x, c: ((z + k) % ZS, y, x, c))

    def shift(self, value, s):
        def move(z, y, x, c):
            to = 2 * z + y + s
            needed = 0 <= to < PIECES and experts_of(2 * z + y) & experts_of(to)
            return (to // 2, to % 2, x, c) if needed else None

        return self.send(value, move)

    def line_groups(self):
        return [
            [self.index(z, y, x, c, team) for z in range(ZS)]
            for team in range(self.teams)
            for y in range(2)
            for x in range(2)
            for c in range(2)
        ]

    def team_groups(self):
        return [
            [self.index(z, y, x, c, team) for team in range(self.teams)]
            for z in range(ZS)
            for y in range(2)
            for x in range(2)
            for c in range(2)
        ]


def turn(place, piece):
    return turn_join(place, turn_send(place, piece))


def turn_send(place, piece):
    upright = piece.T
    twice = jnp.concatenate([upright, upright], axis=0)
    parts = []
    for s in range(REACH, -REACH - 1, -1):
        start = (PIECE_ROWS * (place.piece + s + PIECES)) % D
        tile = lax.dynamic_slice(twice, (start, 0), (PIECE_ROWS, PIECE_ROWS))
        parts.append(place.shift(tile, s) if s else tile)
    return parts


def turn_join(place, parts):
    row = jnp.concatenate(parts, axis=1)
    steps = PIECE_ROWS // STEP
    blocks = []
    for j in range(steps):
        expert = (steps * place.piece + j) // (D // STEP)
        start = STEP * ((D // STEP) * expert - steps * (place.piece - REACH))
        blocks.append(lax.dynamic_slice(row, (STEP * j, start), (STEP, D)))
    return jnp.concatenate(blocks, axis=0)


def block_rows(k):
    low, high = BLOCK * k, BLOCK * (k + 1)
    found = []
    for y in range(2):
        a, b = max(low, PIECE_ROWS * y), min(high, PIECE_ROWS * (y + 1))
        if a < b:
            found.append((y, a - PIECE_ROWS * y, b - PIECE_ROWS * y))
    return found


def block_weight(refs, k):
    return jnp.concatenate(
        [ref[y, x, a:b] for ref in refs for x in range(2) for y, a, b in block_rows(k)], axis=0
    )


def head_scores(packed, block, odd):
    lane = lax.broadcasted_iota(jnp.int32, (TOKENS, LANES), 1)
    mine = (lane >= HEAD_DIM) if odd else (lane < HEAD_DIM)
    queries = packed[:, LANES * block : LANES * (block + 1)]
    queries = jnp.where(mine, queries, jnp.zeros_like(queries))
    keys = packed[:, HALF + LANES * block : HALF + LANES * (block + 1)]
    scores = dot(queries, keys, NT) * (1.0 / math.sqrt(HEAD_DIM))
    column = lax.broadcasted_iota(jnp.int32, (TOKENS, TOKENS), 1)
    scores = jnp.where(column < PATCHES, scores, -1e30)
    powers = jnp.exp(scores - jnp.max(scores, axis=1, keepdims=True))
    exact = powers / jnp.sum(powers, axis=1, keepdims=True)
    return exact, mine, queries, keys


def attention_kernel(pair_ref, norm_ref, weight_ref, first_ref, packed_ref, attended_ref):
    for i in range(2):
        value = pair_ref[i].astype(f32)
        first, _, _ = norm_forward(value, norm_ref[0:1], norm_ref[1:2])
        first = first.astype(bf16)
        first_ref[i] = first
        packed = dot(first, weight_ref[...], NN).astype(bf16)
        packed_ref[i] = packed
        for block in range(HALF // LANES):
            values = packed[:, 2 * HALF + LANES * block : 2 * HALF + LANES * (block + 1)]
            outs = []
            for odd in range(2):
                exact, mine, _, _ = head_scores(packed, block, odd)
                outs.append(dot(exact.astype(bf16), values, NN))
            attended_ref[i, :, LANES * block : LANES * (block + 1)] = jnp.where(
                mine, outs[1], outs[0]
            ).astype(bf16)


def attention_call(pair, norms, weight):
    vmem = pl.BlockSpec(memory_space=pltpu.VMEM)
    return pl.pallas_call(
        attention_kernel,
        out_shape=(
            jax.ShapeDtypeStruct((2, TOKENS, D), bf16),
            jax.ShapeDtypeStruct((2, TOKENS, 3 * HALF), bf16),
            jax.ShapeDtypeStruct((2, TOKENS, HALF), bf16),
        ),
        in_specs=[vmem] * 3,
        out_specs=(vmem,) * 3,
        compiler_params=pltpu.CompilerParams(vmem_limit_bytes=48 * 1024 * 1024),
        cost_estimate=pl.CostEstimate(
            flops=1_100_000_000, bytes_accessed=5_000_000, transcendentals=500_000
        ),
    )(pair, norms, weight)


def attention_back_kernel(
    packed_ref,
    own_grad_ref,
    other_grad_ref,
    first_ref,
    weight_ref,
    own_ref,
    other_ref,
    left_ref,
    right_ref,
    qkv_ref,
    total_ref,
):
    scale = 1.0 / math.sqrt(HEAD_DIM)
    for i, upper_ref in ((1, other_grad_ref), (0, own_grad_ref)):
        packed = packed_ref[i]
        for block in range(HALF // LANES):
            span = slice(LANES * block, LANES * (block + 1))
            values = packed[:, 2 * HALF + LANES * block : 2 * HALF + LANES * (block + 1)]
            upper = upper_ref[:, span]
            found = []
            for odd in range(2):
                exact, mine, queries, keys = head_scores(packed, block, odd)
                masked = jnp.where(mine, upper, jnp.zeros_like(upper))
                prob_grad = dot(masked, values, NT)
                mean = jnp.sum(exact * prob_grad, axis=1, keepdims=True)
                score_grad = (exact * (prob_grad - mean)).astype(bf16)
                found.append(
                    (
                        dot(score_grad, keys, NN) * scale,
                        dot(score_grad, queries, TN) * scale,
                        dot(exact.astype(bf16), masked, TN),
                    )
                )
            for n in range(3):
                qkv_ref[:, HALF * n + LANES * block : HALF * n + LANES * (block + 1)] = jnp.where(
                    mine, found[1][n], found[0][n]
                ).astype(bf16)
        grads = qkv_ref[...]
        back = dot(grads, weight_ref[...], NT)
        if i == 1:
            other_ref[...] = back.astype(bf16)
            total_ref[...] = dot(first_ref[i], grads, TN)
        else:
            own_ref[...] = back
    total = total_ref[...] + dot(first_ref[0], grads, TN)
    left_ref[...] = total[:, :D].astype(bf16)
    right_ref[...] = total[:, D:].astype(bf16)


def attention_back_call(after, *operands):
    vmem = pl.BlockSpec(memory_space=pltpu.VMEM)
    return pl.pallas_call(
        follow(attention_back_kernel, len(after), len(operands)),
        out_shape=(
            jax.ShapeDtypeStruct((TOKENS, D), f32),
            jax.ShapeDtypeStruct((TOKENS, D), bf16),
            jax.ShapeDtypeStruct((D, D), bf16),
            jax.ShapeDtypeStruct((D, HALF), bf16),
        ),
        in_specs=[vmem] * len(operands) + [pl.BlockSpec(memory_space=pl.ANY)] * len(after),
        out_specs=(vmem,) * 4,
        scratch_shapes=[
            pltpu.VMEM((TOKENS, 3 * HALF), bf16),
            pltpu.VMEM((D, 3 * HALF), f32),
        ],
        compiler_params=pltpu.CompilerParams(vmem_limit_bytes=48 * 1024 * 1024),
        cost_estimate=pl.CostEstimate(
            flops=2_500_000_000, bytes_accessed=8_000_000, transcendentals=500_000
        ),
    )(*operands, *after)


def find_gates(second, router, codes_ref):
    lane = lax.broadcasted_iota(jnp.int32, (TOKENS, LANES), 1)
    token = lax.broadcasted_iota(jnp.int32, (TOKENS, SLOTS), 0)
    there = jnp.zeros((TOKENS, LANES), f32)
    for e in range(EXPERTS):
        match = (token == codes_ref[e : e + 1, :]).astype(f32)
        there = jnp.where(lane == e, jnp.max(match, axis=1, keepdims=True), there)
    logits = dot(second, router, NN)
    masked = jnp.where(there > 0, logits, -1e30)
    peak = jnp.max(masked, axis=1, keepdims=True)
    weight = jnp.where(there > 0, jnp.exp(masked - peak), 0.0)
    total = jnp.sum(weight, axis=1, keepdims=True)
    return weight / jnp.where(total > 0, total, 1.0)


def middle_kernel(
    core_ref, mine_ref, other_ref, image_ref, own_w, other_w, norm_ref, middle_ref, second_ref
):
    core = core_ref[0]
    here, there = (pl.multiple_of(HALF * c, LANES) for c in (core, 1 - core))
    for columns, w in ((here, own_w), (there, other_w)):
        middle_ref[:, pl.ds(columns, HALF)] = dot(
            mine_ref[...], w[pl.ds(here, HALF), :], NN
        ) + dot(other_ref[...], w[pl.ds(there, HALF), :], NN)
    middle = image_ref[...].astype(f32) + middle_ref[...] + norm_ref[2:3]
    middle_ref[...] = middle
    second, _, _ = norm_forward(middle, norm_ref[0:1], norm_ref[1:2])
    second_ref[...] = second.astype(bf16)


def middle_call(core, mine, other, image, own_w, other_w, norms):
    vmem = pl.BlockSpec(memory_space=pltpu.VMEM)
    return pl.pallas_call(
        middle_kernel,
        out_shape=(
            jax.ShapeDtypeStruct((TOKENS, D), f32),
            jax.ShapeDtypeStruct((TOKENS, D), bf16),
        ),
        in_specs=[pl.BlockSpec(memory_space=pltpu.SMEM)] + [vmem] * 6,
        out_specs=(vmem,) * 2,
        compiler_params=pltpu.CompilerParams(vmem_limit_bytes=32 * 1024 * 1024),
        cost_estimate=pl.CostEstimate(
            flops=250_000_000, bytes_accessed=3_500_000, transcendentals=0
        ),
    )(core, mine, other, image, own_w, other_w, norms)


def middle_back_kernel(
    core_ref,
    back0_ref,
    back1_ref,
    back2_ref,
    back3_ref,
    second_ref,
    middle_ref,
    dy_ref,
    router_ref,
    own_w,
    other_w,
    norm_ref,
    mine_ref,
    other_ref,
    grad_ref,
    mine_grad_ref,
    other_grad_ref,
    own_cols_ref,
    other_cols_ref,
    vector_ref,
    router_grad_ref,
    total_ref,
    spare_ref,
    codes_ref,
    proj_ref,
):
    core = core_ref[0]
    here, there = (pl.multiple_of(HALF * c, LANES) for c in (core, 1 - core))
    total_ref[...] = (
        back0_ref[...].astype(f32)
        + back1_ref[...].astype(f32)
        + back2_ref[...].astype(f32)
        + back3_ref[...].astype(f32)
    )
    codes_ref[...] = dy_ref[EXTRA:, :SLOTS].astype(f32).astype(jnp.int32)
    lane = lax.broadcasted_iota(jnp.int32, (TOKENS, LANES), 1)
    real = lax.broadcasted_iota(jnp.int32, (TOKENS, D), 0) < PATCHES
    second = second_ref[...]
    gates = find_gates(second, router_ref[...], codes_ref)
    spare_ref[...] = jnp.zeros_like(spare_ref)
    spare = total_ref[EXTRA:, : 2 * LANES]
    spare_ref[:8] = spare + pltpu.roll(spare, 4, 0)
    gate_grad = jnp.where(lane < EXPERTS, spare_ref[...].T[:TOKENS], 0.0)
    mean = jnp.sum(gates * gate_grad, axis=1, keepdims=True)
    logit_grad = (gates * (gate_grad - mean)).astype(bf16)
    second_grad = total_ref[...] + dot(logit_grad, router_ref[...], NT)
    second_grad = jnp.where(real, second_grad, 0.0)
    router_grad_ref[...] = dot(second, logit_grad, TN)
    _, unit, inverse = norm_forward(middle_ref[...], norm_ref[0:1], norm_ref[1:2])
    back, gain_grad, bias_grad = norm_backward(second_grad, unit, inverse, norm_ref[0:1])
    middle_grad = jnp.where(real, dy_ref[...].astype(f32) + back, 0.0)
    grad_ref[...] = middle_grad
    vector_ref[...] = jnp.zeros_like(vector_ref)
    vector_ref[0:1] = gain_grad[None]
    vector_ref[1:2] = bias_grad[None]
    vector_ref[2:3] = jnp.sum(middle_grad, axis=0)[None]
    proj_ref[...] = middle_grad.astype(bf16)
    own = proj_ref[:, pl.ds(here, HALF)]
    other = proj_ref[:, pl.ds(there, HALF)]
    for rows, out_ref in ((here, mine_grad_ref), (there, other_grad_ref)):
        out_ref[...] = (
            dot(own, own_w[pl.ds(rows, HALF), :], NT) + dot(other, other_w[pl.ds(rows, HALF), :], NT)
        ).astype(bf16)
    for columns, out_ref in ((own, own_cols_ref), (other, other_cols_ref)):
        out_ref[pl.ds(here, HALF), :] = dot(mine_ref[...], columns, TN).astype(bf16)
        out_ref[pl.ds(there, HALF), :] = dot(other_ref[...], columns, TN).astype(bf16)


def middle_back_call(after, core, *operands):
    vmem = pl.BlockSpec(memory_space=pltpu.VMEM)
    return pl.pallas_call(
        follow(middle_back_kernel, len(after), 1 + len(operands)),
        out_shape=(
            jax.ShapeDtypeStruct((TOKENS, D), f32),
            jax.ShapeDtypeStruct((TOKENS, HALF), bf16),
            jax.ShapeDtypeStruct((TOKENS, HALF), bf16),
            jax.ShapeDtypeStruct((D, HALF), bf16),
            jax.ShapeDtypeStruct((D, HALF), bf16),
            jax.ShapeDtypeStruct((8, D), f32),
            jax.ShapeDtypeStruct((D, LANES), f32),
        ),
        in_specs=[pl.BlockSpec(memory_space=pltpu.SMEM)]
        + [vmem] * len(operands)
        + [pl.BlockSpec(memory_space=pl.ANY)] * len(after),
        out_specs=(vmem,) * 7,
        scratch_shapes=[
            pltpu.VMEM((TOKENS, D), f32),
            pltpu.VMEM((LANES, 2 * LANES), f32),
            pltpu.VMEM((TOKENS - EXTRA, SLOTS), jnp.int32),
            pltpu.VMEM((TOKENS, D), bf16),
        ],
        compiler_params=pltpu.CompilerParams(vmem_limit_bytes=48 * 1024 * 1024),
        cost_estimate=pl.CostEstimate(
            flops=800_000_000, bytes_accessed=8_000_000, transcendentals=0
        ),
    )(core, *operands, *after)


def follow(kernel, count, n_in):
    def wrapped(*refs):
        return kernel(*refs[:n_in], *refs[n_in + count :])

    return wrapped


def last_kernel(own_ref, arrived_ref, image_ref, norm_ref, middle_grad_ref, grad_ref, vector_ref):
    incoming = own_ref[...] + arrived_ref[...].astype(f32)
    real = lax.broadcasted_iota(jnp.int32, (TOKENS, D), 0) < PATCHES
    incoming = jnp.where(real, incoming, 0.0)
    _, unit, inverse = norm_forward(image_ref[...].astype(f32), norm_ref[0:1], norm_ref[1:2])
    back, gain_grad, bias_grad = norm_backward(incoming, unit, inverse, norm_ref[0:1])
    grad_ref[...] = (middle_grad_ref[...] + back).astype(bf16)
    vector_ref[...] = jnp.zeros_like(vector_ref)
    vector_ref[0:1] = gain_grad[None]
    vector_ref[1:2] = bias_grad[None]


def last_call(after, *operands):
    vmem = pl.BlockSpec(memory_space=pltpu.VMEM)
    return pl.pallas_call(
        follow(last_kernel, len(after), len(operands)),
        out_shape=(
            jax.ShapeDtypeStruct((TOKENS, D), bf16),
            jax.ShapeDtypeStruct((8, D), f32),
        ),
        in_specs=[vmem] * len(operands) + [pl.BlockSpec(memory_space=pl.ANY)] * len(after),
        out_specs=(vmem,) * 2,
        compiler_params=pltpu.CompilerParams(vmem_limit_bytes=24 * 1024 * 1024),
        cost_estimate=pl.CostEstimate(flops=2_000_000, bytes_accessed=2_500_000, transcendentals=0),
    )(*operands, *after)


def image_kernel(
    expert_ref,
    second_ref,
    dy_ref,
    router_ref,
    own_in_ref,
    other_in_ref,
    own_back_ref,
    other_back_ref,
    back_ref,
    mix_ref,
    rows_ref,
    grads_ref,
    active_ref,
    hidden_grad_ref,
    back_sum,
    gate_sum,
    mix_sum,
    codes_ref,
):
    lane = lax.broadcasted_iota(jnp.int32, (TOKENS, LANES), 1)
    token = lax.broadcasted_iota(jnp.int32, (TOKENS, SLOTS), 0)
    codes_ref[...] = dy_ref[EXTRA:, :SLOTS].astype(f32).astype(jnp.int32)
    gates = find_gates(second_ref[...], router_ref[...], codes_ref)
    gate_sum[...] = jnp.zeros_like(gate_sum)
    for k in range(BLOCKS):
        expert = expert_ref[k]
        w_in = block_weight((own_in_ref, other_in_ref), k)
        w_back = block_weight((own_back_ref, other_back_ref), k)
        placing = (token == codes_ref[pl.ds(expert, 1), :]).astype(f32).astype(bf16)
        gate = jnp.sum(jnp.where(lane == expert, gates, 0.0), axis=1, keepdims=True)
        rows = dot(placing, second_ref[...], TN).astype(bf16)
        scaled = (dy_ref[...].astype(f32) * gate).astype(bf16)
        grads = dot(placing, scaled, TN).astype(bf16)
        rows_ref[k] = rows
        grads_ref[k] = grads
        hidden = dot(rows, w_in, NT)
        phi = 0.5 * (1.0 + lax.erf(hidden * (1.0 / math.sqrt(2.0))))
        active = (hidden * phi).astype(bf16)
        slope = phi + hidden * jnp.exp(-0.5 * hidden * hidden) * (1.0 / math.sqrt(2.0 * math.pi))
        active_ref[k] = active
        hidden_grad = (dot(grads, w_back, NT) * slope).astype(bf16)
        hidden_grad_ref[k] = hidden_grad
        produced = dot(active, w_back, NN).astype(bf16)
        rows_grad = dot(hidden_grad, w_in, NN).astype(bf16)
        output = dot(placing, produced, NN)
        gate_grad = jnp.sum(output * dy_ref[...].astype(f32), axis=1, keepdims=True)
        gate_sum[:TOKENS] += jnp.where(lane == expert, gate_grad, 0.0)
        if k == 0:
            back_sum[...] = dot(placing, rows_grad, NN)
            mix_sum[...] = output * gate
        else:
            back_sum[...] += dot(placing, rows_grad, NN)
            mix_sum[...] += output * gate
    spare = gate_sum[...].T[:8]
    high = spare.astype(bf16).astype(f32)
    low = (spare - high).astype(bf16).astype(f32)
    row = lax.broadcasted_iota(jnp.int32, spare.shape, 0)
    back_sum[EXTRA:, : 2 * LANES] = jnp.where(row < 4, high, pltpu.roll(low, 4, 0))
    back_ref[...] = back_sum[...].astype(bf16)
    mix_ref[...] = mix_sum[...].astype(bf16)


def image_call(after, experts, second, dy, router, *weights):
    vmem = pl.BlockSpec(memory_space=pltpu.VMEM)
    return pl.pallas_call(
        follow(image_kernel, len(after), 8),
        out_shape=(
            jax.ShapeDtypeStruct((TOKENS, D), bf16),
            jax.ShapeDtypeStruct((TOKENS, D), bf16),
            jax.ShapeDtypeStruct((BLOCKS, SLOTS, D), bf16),
            jax.ShapeDtypeStruct((BLOCKS, SLOTS, D), bf16),
            jax.ShapeDtypeStruct((BLOCKS, SLOTS, WIDE), bf16),
            jax.ShapeDtypeStruct((BLOCKS, SLOTS, WIDE), bf16),
        ),
        in_specs=[pl.BlockSpec(memory_space=pltpu.SMEM)]
        + [vmem] * 7
        + [pl.BlockSpec(memory_space=pl.ANY)] * len(after),
        out_specs=(vmem,) * 6,
        scratch_shapes=[
            pltpu.VMEM((TOKENS, D), f32),
            pltpu.VMEM((2 * LANES, LANES), f32),
            pltpu.VMEM((TOKENS, D), f32),
            pltpu.VMEM((TOKENS - EXTRA, SLOTS), jnp.int32),
        ],
        compiler_params=pltpu.CompilerParams(vmem_limit_bytes=48 * 1024 * 1024),
        cost_estimate=pl.CostEstimate(
            flops=1, bytes_accessed=1, transcendentals=0
        ),
    )(experts, second, dy, router, *weights, *after)


def weight_kernel(*refs):
    lefts, rights, outs = refs[:ZS], refs[ZS : 2 * ZS], refs[2 * ZS :]
    for half, out_ref in zip((1, 0), outs):
        span = slice(half * WIDE // 2, (half + 1) * WIDE // 2)
        for k in range(BLOCKS):
            total = dot(lefts[0][k, :, span], rights[0][k], TN)
            for n in range(1, ZS):
                total += dot(lefts[n][k, :, span], rights[n][k], TN)
            done = 0
            for x in range(2):
                for y, a, b in block_rows(k):
                    out_ref[y, x, a:b] = total[done : done + b - a].astype(bf16)
                    done += b - a


def weight_call(after, *operands):
    vmem = pl.BlockSpec(memory_space=pltpu.VMEM)
    return pl.pallas_call(
        follow(weight_kernel, len(after), len(operands)),
        out_shape=(jax.ShapeDtypeStruct((2, 2, PIECE_ROWS, D), bf16),) * 2,
        in_specs=[vmem] * len(operands) + [pl.BlockSpec(memory_space=pl.ANY)] * len(after),
        out_specs=(vmem,) * 2,
        compiler_params=pltpu.CompilerParams(vmem_limit_bytes=48 * 1024 * 1024),
        cost_estimate=pl.CostEstimate(
            flops=4_100_000_000, bytes_accessed=9_000_000, transcendentals=0
        ),
    )(*operands, *after)


def pick(value, index, axis=0):
    return lax.dynamic_index_in_dim(value, index, axis, keepdims=False)


def add_rows(kept, got):
    return (kept.astype(f32) + got.astype(f32)).astype(bf16)


def scatter_parts(place, value):
    m = place.teams
    value = value.reshape(4, 2, m, 2, 2 * D // (TEAM * m), -1)
    return value.transpose(0, 1, 3, 2, 4, 5).reshape(4, 2, 2, 2 * D // TEAM, -1)


def scatter_rows(place, left, right, held):
    m = place.teams
    each = D // (TEAM * m)

    def fold(part, axis, side):
        here, move = (place.x, (0, 1)) if axis == "x" else (place.y, (1, 0))
        return add_rows(pick(part, here, side), place.flip(pick(part, 1 - here, side), *move))

    right = fold(scatter_parts(place, right), "y", 1)
    left, right, held = lax.optimization_barrier((left, right, held))
    left, right = fold(left, "y", 1), fold(right, "x", 1)
    both = jnp.concatenate([left, right], axis=-1)
    total = pick(both, place.z).astype(f32)
    for k in range(1, ZS):
        total += place.roll(pick(both, (place.z + k) % ZS), k).astype(f32)
    total = total.reshape(m, 2 * each, -1)
    if m > 1:
        total = lax.psum_scatter(
            total, "fsdp", scatter_dimension=0, axis_index_groups=place.team_groups()
        )
    return total.reshape(2, each, -1), held


def in_order(index, mine, other, axis):
    first = index == 0
    return jnp.stack([jnp.where(first, mine, other), jnp.where(first, other, mine)], axis=axis)


def by_core(place, mine, other):
    first = place.core == 0
    return jnp.stack([jnp.where(first, mine, other), jnp.where(first, other, mine)], axis=-2)


def local(images, slots, small_params, qkv_weight, out_weight, expert_in, expert_out, cotangent):
    place = Place()
    teams = place.teams
    each = D // (TEAM * teams)
    core = place.core
    qkv_rows = qkv_weight.reshape(each, 3, 2, HALF)
    out_rows = out_weight.reshape(each, 2, HALF)
    small_rows = jnp.pad(small_params.reshape(each, 8), ((0, 0), (0, LANES - 8)))

    def half_rows(c):
        return jnp.concatenate(
            [pick(qkv_rows, c, 2).reshape(each, 3 * HALF), small_rows, pick(out_rows, c, 1)], axis=1
        )

    layer = in_order(core, half_rows(core), place.swap_core(half_rows(1 - core)), 0)
    layer = lax.all_gather(
        layer.reshape(2 * each, -1),
        "fsdp",
        axis=0,
        tiled=True,
        axis_index_groups=[list(range(c, teams * TEAM, 2)) for c in range(2)],
    )
    piece_in, piece_back = expert_in.reshape(-1, D), expert_out.reshape(-1, D)
    if teams > 1:
        piece_in, piece_back = (
            lax.all_gather(
                piece, "fsdp", axis=0, tiled=True, axis_index_groups=place.team_groups()
            )
            for piece in (piece_in, piece_back)
        )

    codes = jnp.where(slots[0] >= 0, slots[0] // 2, -1)
    dy_own = jnp.pad(cotangent[0], ((0, EXTRA - PATCHES), (0, 0)))
    spare = jnp.pad(
        codes, ((0, TOKENS - EXTRA - EXPERTS), (0, D - CAP)), constant_values=-1
    ).astype(bf16)
    dy_own = jnp.concatenate([dy_own, spare], axis=0)

    in_parts = turn_send(place, piece_in)
    dy_own, in_parts = lax.optimization_barrier((dy_own, in_parts))
    dy_moved = {k: place.roll(dy_own, k) if k else dy_own for k in (0, 1, 3, 2)}
    turned = turn_join(place, in_parts)
    moves = ((0, 0), (0, 1), (1, 0), (1, 1))
    weights = ()
    for piece in (turned, piece_back):
        pieces = [place.flip(piece, *move) if any(move) else piece for move in moves]
        if piece is turned:
            pieces, dy_moved = lax.optimization_barrier((pieces, dy_moved))
        own = in_order(place.y, jnp.stack(pieces[:2]), jnp.stack(pieces[2:]), 0)
        weights += (own, place.swap_core(own))

    image = images[0]
    inputs = image.astype(f32)
    pair = jnp.stack([image, place.swap_core(image)])
    pair = jnp.pad(pair, ((0, 0), (0, TOKENS - PATCHES), (0, 0)))
    w_qkv = layer[:, : 3 * HALF]
    small = layer[:, 3 * HALF : 3 * HALF + 8].reshape(-1)
    out_own = layer[:, 3 * HALF + LANES :]
    out_other = place.swap_core(out_own)

    gain_one, bias_one, gain_two, bias_two, bias_out = (
        small[n * D : (n + 1) * D].astype(f32) for n in range(5)
    )
    router = jnp.pad(small[5 * D :].reshape(D, EXPERTS), ((0, 0), (0, LANES - EXPERTS)))
    norms = jnp.stack([gain_one, bias_one])
    first, packed, attended_part = attention_call(pair, norms, w_qkv)
    attended_other = place.swap_core(attended_part[1])
    core_index = core[None].astype(jnp.int32)
    norms_two = jnp.stack([gain_two, bias_two, bias_out])
    middle, second_own = middle_call(
        core_index, attended_part[0], attended_other, pair[0], out_own, out_other, norms_two
    )

    experts = (BLOCKS * place.z + jnp.arange(BLOCKS, dtype=jnp.int32)) // ZS
    moved = {k: place.roll(second_own, k) for k in (1, 3, 2)}
    moved[0] = second_own
    results = {}
    returned = {}
    for k in (0, 1, 3, 2):
        after = [returned[n] for n in list(returned)[:-1][-1:] if n]
        if results:
            after.append(before)
        results[k] = image_call(after, experts, moved[k], dy_moved[k], router, *weights)
        before = results[k][0]
        returned[k] = place.roll(before, -k) if k else before
    rows, grads, active, hidden_grad = zip(*(result[2:] for result in results.values()))

    def chip_sum(other, own):
        return (own.astype(f32) + place.swap_core(other).astype(f32)).astype(bf16)

    def spread(chip):
        here, there = pick(chip, place.y), pick(chip, 1 - place.y)
        return [
            here[0],
            place.flip(here[1], 0, 1),
            place.flip(there[0], 1, 0),
            place.flip(there[1], 1, 1),
        ]

    in_other, in_own = weight_call([], *hidden_grad, *rows)
    back_other, back_own = weight_call([in_own, returned[2]], *active, *grads)
    in_chip = chip_sum(in_other, in_own)
    in_moved = spread(in_chip)
    back_chip = chip_sum(back_other, back_own)
    back_moved = spread(back_chip)
    (
        middle_grad,
        mine_grad,
        other_grad,
        proj_own,
        proj_other,
        vectors,
        router_grad,
    ) = middle_back_call(
        [in_chip, back_chip],
        core_index,
        *returned.values(),
        second_own,
        middle,
        dy_own,
        router,
        out_own,
        out_other,
        norms_two,
        attended_part[0],
        attended_other,
    )
    arrived_grad = place.swap_core(other_grad)
    proj_arrived = place.swap_core(proj_other)

    in_parts = turn_send(place, sum(part.astype(f32) for part in in_moved).astype(bf16))
    first_grad, other_grad, qk_grad, v_grad = attention_back_call(
        in_moved[1:] + back_moved[1:], packed, mine_grad, arrived_grad, first, w_qkv
    )
    mixed = [results[k][1] for k in range(ZS - 1, -1, -1)]
    mixed = lax.dynamic_slice_in_dim(jnp.stack(mixed + mixed), ZS - 1 - place.z, ZS, 0)
    mixed, v_grad = lax.optimization_barrier((mixed, v_grad))
    mixture = lax.psum_scatter(
        mixed, "fsdp", scatter_dimension=0, axis_index_groups=place.line_groups()
    )
    qk_parts = scatter_parts(place, qk_grad)
    sent, in_parts = lax.optimization_barrier((pick(qk_parts, 1 - place.x, 2), in_parts))
    qk_got = place.flip(sent, 0, 1)
    input_grad, vectors_one = last_call(
        [], first_grad, place.swap_core(other_grad), pair[0], norms, middle_grad
    )
    input_grad = input_grad[:PATCHES]
    small_terms = jnp.concatenate(
        [
            vectors_one[:2].reshape(-1),
            vectors[:3].reshape(-1),
            router_grad[:, :EXPERTS].reshape(-1),
        ]
    )
    small_terms = small_terms.astype(bf16).reshape(TEAM * teams, -1)
    length = -(-small_terms.shape[1] // LANES)
    small_terms = jnp.pad(
        small_terms, ((0, 0), (0, length * LANES - small_terms.shape[1]))
    ).reshape(TEAM * teams, length, LANES)
    small_terms = jnp.pad(small_terms, ((0, 0), (0, each - length), (0, 0))).reshape(D, LANES)
    proj_grad = (proj_own.astype(f32) + proj_arrived.astype(f32)).astype(bf16)
    rows, back_moved = scatter_rows(
        place,
        add_rows(pick(qk_parts, place.x, 2), qk_got),
        jnp.concatenate([v_grad, proj_grad, small_terms], axis=1),
        back_moved,
    )
    mine = pick(rows, core)
    other = place.swap_core(pick(rows, 1 - core).astype(bf16)).astype(f32)

    def joined(a, b, count):
        cut = [half[:, a:b].reshape(each, count, -1) for half in (mine, other)]
        return by_core(place, *cut).reshape(-1)

    small_grad = mine[:length, 4 * HALF :] + other[:length, 4 * HALF :]
    small_grad = small_grad.reshape(-1)[: 8 * each]
    qkv_weight_grad = joined(0, 3 * HALF, 3)
    out_weight_grad = joined(3 * HALF, 4 * HALF, 1)
    block_output = (middle + mixture.astype(f32))[:PATCHES].astype(bf16)
    in_grad = turn_join(place, in_parts).astype(f32)
    back_grad = sum(part.astype(f32) for part in back_moved)
    if teams > 1:
        in_grad, back_grad = (
            lax.psum_scatter(
                grad,
                "fsdp",
                scatter_dimension=0,
                tiled=True,
                axis_index_groups=place.team_groups(),
            )
            for grad in (in_grad, back_grad)
        )
    return (
        block_output[None],
        input_grad[None],
        small_grad,
        qkv_weight_grad,
        out_weight_grad,
        in_grad.reshape(-1),
        back_grad.reshape(-1),
    )


def solution(mesh):
    rows = P("fsdp", None, None)
    flat = P("fsdp")
    return jax.shard_map(
        local,
        mesh=mesh,
        in_specs=(rows, rows, flat, flat, flat, flat, flat, rows),
        out_specs=(rows, rows, flat, flat, flat, flat, flat),
        check_vma=False,
    )
```

```python
import functools
import math

import jax
import jax.numpy as jnp
from jax import lax
from jax.experimental import pallas as pl
from jax.experimental.pallas import tpu as pltpu
from jax.sharding import PartitionSpec as P

D = 768
HEADS = 12
HEAD_DIM = 64
EXPERTS = 3
GROUP = 4
PATCHES = 197
CAP = 136
EPSILON = 1e-06

ZS = 4
TEAM = 32
PIECES = TEAM // GROUP
PIECE_ROWS = EXPERTS * D // PIECES
STEP = 96
REACH = 3
BLOCK = 192
BLOCKS = 3
WIDE = GROUP * BLOCK
TOKENS = 208
EXTRA = 200
SLOTS = 144
LANES = 128
HALF = D // 2

f32 = jnp.float32
bf16 = jnp.bfloat16


def norm_forward(value, gain, bias):
    average = jnp.mean(value, axis=-1, keepdims=True)
    centred = value - average
    inverse = lax.rsqrt(jnp.mean(centred * centred, axis=-1, keepdims=True) + EPSILON)
    normed = centred * inverse
    return normed * gain + bias, normed, inverse


def norm_backward(incoming, normed, inverse, gain):
    scaled = incoming * gain
    returned = inverse * (
        scaled
        - jnp.mean(scaled, axis=-1, keepdims=True)
        - normed * jnp.mean(scaled * normed, axis=-1, keepdims=True)
    )
    return returned, jnp.sum(incoming * normed, axis=0), jnp.sum(incoming, axis=0)


def dot(a, b, dims):
    return lax.dot_general(a, b, (dims, ((), ())), preferred_element_type=f32)


NN = ((1,), (0,))
NT = ((1,), (1,))
TN = ((0,), (0,))


def experts_of(piece):
    steps = PIECE_ROWS // STEP
    return {(steps * piece + j) // (D // STEP) for j in range(steps)}


class Place:
    def __init__(self):
        self.teams = lax.axis_size("fsdp") // TEAM
        index = lax.axis_index("fsdp")
        self.core = index % 2
        self.x = (index // 2) % 2
        self.piece = index // (GROUP * self.teams)
        self.y = self.piece % 2
        self.z = self.piece // 2

    def index(self, z, y, x, core, team):
        return ((2 * z + y) * self.teams + team) * GROUP + 2 * x + core

    def send(self, value, move):
        pairs = []
        for team in range(self.teams):
            for z in range(ZS):
                for y in range(2):
                    for x in range(2):
                        for core in range(2):
                            to = move(z, y, x, core)
                            if to is not None:
                                pairs.append(
                                    (self.index(z, y, x, core, team), self.index(*to, team))
                                )
        return lax.ppermute(value, "fsdp", pairs)

    def swap_core(self, value):
        return self.send(value, lambda z, y, x, c: (z, y, x, 1 - c))

    def flip(self, value, dy, dx):
        return self.send(value, lambda z, y, x, c: (z, y ^ dy, x ^ dx, c))

    def roll(self, value, k):
        return self.send(value, lambda z, y, x, c: ((z + k) % ZS, y, x, c))

    def shift(self, value, s):
        def move(z, y, x, c):
            to = 2 * z + y + s
            needed = 0 <= to < PIECES and experts_of(2 * z + y) & experts_of(to)
            return (to // 2, to % 2, x, c) if needed else None

        return self.send(value, move)

    def line_groups(self):
        return [
            [self.index(z, y, x, c, team) for z in range(ZS)]
            for team in range(self.teams)
            for y in range(2)
            for x in range(2)
            for c in range(2)
        ]

    def team_groups(self):
        return [
            [self.index(z, y, x, c, team) for team in range(self.teams)]
            for z in range(ZS)
            for y in range(2)
            for x in range(2)
            for c in range(2)
        ]


def turn(place, piece):
    return turn_join(place, turn_send(place, piece))


def turn_send(place, piece):
    upright = piece.T
    twice = jnp.concatenate([upright, upright], axis=0)
    parts = []
    for s in range(REACH, -REACH - 1, -1):
        start = (PIECE_ROWS * (place.piece + s + PIECES)) % D
        tile = lax.dynamic_slice(twice, (start, 0), (PIECE_ROWS, PIECE_ROWS))
        parts.append(place.shift(tile, s) if s else tile)
    return parts


def turn_join(place, parts):
    row = jnp.concatenate(parts, axis=1)
    steps = PIECE_ROWS // STEP
    blocks = []
    for j in range(steps):
        expert = (steps * place.piece + j) // (D // STEP)
        start = STEP * ((D // STEP) * expert - steps * (place.piece - REACH))
        blocks.append(lax.dynamic_slice(row, (STEP * j, start), (STEP, D)))
    return jnp.concatenate(blocks, axis=0)


def block_rows(k):
    low, high = BLOCK * k, BLOCK * (k + 1)
    found = []
    for y in range(2):
        a, b = max(low, PIECE_ROWS * y), min(high, PIECE_ROWS * (y + 1))
        if a < b:
            found.append((y, a - PIECE_ROWS * y, b - PIECE_ROWS * y))
    return found


def block_weight(refs, k):
    return jnp.concatenate(
        [ref[y, x, a:b] for ref in refs for x in range(2) for y, a, b in block_rows(k)], axis=0
    )


def head_scores(packed, block, odd):
    lane = lax.broadcasted_iota(jnp.int32, (TOKENS, LANES), 1)
    mine = (lane >= HEAD_DIM) if odd else (lane < HEAD_DIM)
    queries = packed[:, LANES * block : LANES * (block + 1)]
    queries = jnp.where(mine, queries, jnp.zeros_like(queries))
    keys = packed[:, HALF + LANES * block : HALF + LANES * (block + 1)]
    scores = dot(queries, keys, NT) * (1.0 / math.sqrt(HEAD_DIM))
    column = lax.broadcasted_iota(jnp.int32, (TOKENS, TOKENS), 1)
    scores = jnp.where(column < PATCHES, scores, -1e30)
    powers = jnp.exp(scores - jnp.max(scores, axis=1, keepdims=True))
    exact = powers / jnp.sum(powers, axis=1, keepdims=True)
    return exact, mine, queries, keys


def attention_kernel(pair_ref, norm_ref, weight_ref, first_ref, packed_ref, attended_ref):
    for i in range(2):
        value = pair_ref[i].astype(f32)
        first, _, _ = norm_forward(value, norm_ref[0:1], norm_ref[1:2])
        first = first.astype(bf16)
        first_ref[i] = first
        packed = dot(first, weight_ref[...], NN).astype(bf16)
        packed_ref[i] = packed
        for block in range(HALF // LANES):
            values = packed[:, 2 * HALF + LANES * block : 2 * HALF + LANES * (block + 1)]
            outs = []
            for odd in range(2):
                exact, mine, _, _ = head_scores(packed, block, odd)
                outs.append(dot(exact.astype(bf16), values, NN))
            attended_ref[i, :, LANES * block : LANES * (block + 1)] = jnp.where(
                mine, outs[1], outs[0]
            ).astype(bf16)


def attention_call(pair, norms, weight):
    vmem = pl.BlockSpec(memory_space=pltpu.VMEM)
    return pl.pallas_call(
        attention_kernel,
        out_shape=(
            jax.ShapeDtypeStruct((2, TOKENS, D), bf16),
            jax.ShapeDtypeStruct((2, TOKENS, 3 * HALF), bf16),
            jax.ShapeDtypeStruct((2, TOKENS, HALF), bf16),
        ),
        in_specs=[vmem] * 3,
        out_specs=(vmem,) * 3,
        compiler_params=pltpu.CompilerParams(vmem_limit_bytes=48 * 1024 * 1024),
        cost_estimate=pl.CostEstimate(
            flops=1_100_000_000, bytes_accessed=5_000_000, transcendentals=500_000
        ),
    )(pair, norms, weight)


def attention_back_kernel(
    packed_ref,
    own_grad_ref,
    other_grad_ref,
    first_ref,
    weight_ref,
    own_ref,
    other_ref,
    left_ref,
    right_ref,
    qkv_ref,
    total_ref,
):
    scale = 1.0 / math.sqrt(HEAD_DIM)
    for i, upper_ref in ((1, other_grad_ref), (0, own_grad_ref)):
        packed = packed_ref[i]
        for block in range(HALF // LANES):
            span = slice(LANES * block, LANES * (block + 1))
            values = packed[:, 2 * HALF + LANES * block : 2 * HALF + LANES * (block + 1)]
            upper = upper_ref[:, span]
            found = []
            for odd in range(2):
                exact, mine, queries, keys = head_scores(packed, block, odd)
                masked = jnp.where(mine, upper, jnp.zeros_like(upper))
                prob_grad = dot(masked, values, NT)
                mean = jnp.sum(exact * prob_grad, axis=1, keepdims=True)
                score_grad = (exact * (prob_grad - mean)).astype(bf16)
                found.append(
                    (
                        dot(score_grad, keys, NN) * scale,
                        dot(score_grad, queries, TN) * scale,
                        dot(exact.astype(bf16), masked, TN),
                    )
                )
            for n in range(3):
                qkv_ref[:, HALF * n + LANES * block : HALF * n + LANES * (block + 1)] = jnp.where(
                    mine, found[1][n], found[0][n]
                ).astype(bf16)
        grads = qkv_ref[...]
        back = dot(grads, weight_ref[...], NT)
        if i == 1:
            other_ref[...] = back.astype(bf16)
            total_ref[...] = dot(first_ref[i], grads, TN)
        else:
            own_ref[...] = back
    total = total_ref[...] + dot(first_ref[0], grads, TN)
    left_ref[...] = total[:, :D].astype(bf16)
    right_ref[...] = total[:, D:].astype(bf16)


def attention_back_call(after, *operands):
    vmem = pl.BlockSpec(memory_space=pltpu.VMEM)
    return pl.pallas_call(
        follow(attention_back_kernel, len(after), len(operands)),
        out_shape=(
            jax.ShapeDtypeStruct((TOKENS, D), f32),
            jax.ShapeDtypeStruct((TOKENS, D), bf16),
            jax.ShapeDtypeStruct((D, D), bf16),
            jax.ShapeDtypeStruct((D, HALF), bf16),
        ),
        in_specs=[vmem] * len(operands) + [pl.BlockSpec(memory_space=pl.ANY)] * len(after),
        out_specs=(vmem,) * 4,
        scratch_shapes=[
            pltpu.VMEM((TOKENS, 3 * HALF), bf16),
            pltpu.VMEM((D, 3 * HALF), f32),
        ],
        compiler_params=pltpu.CompilerParams(vmem_limit_bytes=48 * 1024 * 1024),
        cost_estimate=pl.CostEstimate(
            flops=2_500_000_000, bytes_accessed=8_000_000, transcendentals=500_000
        ),
    )(*operands, *after)


def find_gates(second, router, codes_ref):
    lane = lax.broadcasted_iota(jnp.int32, (TOKENS, LANES), 1)
    token = lax.broadcasted_iota(jnp.int32, (TOKENS, SLOTS), 0)
    there = jnp.zeros((TOKENS, LANES), f32)
    for e in range(EXPERTS):
        match = (token == codes_ref[e : e + 1, :]).astype(f32)
        there = jnp.where(lane == e, jnp.max(match, axis=1, keepdims=True), there)
    logits = dot(second, router, NN)
    masked = jnp.where(there > 0, logits, -1e30)
    peak = jnp.max(masked, axis=1, keepdims=True)
    weight = jnp.where(there > 0, jnp.exp(masked - peak), 0.0)
    total = jnp.sum(weight, axis=1, keepdims=True)
    return weight / jnp.where(total > 0, total, 1.0)


def middle_kernel(
    core_ref, mine_ref, other_ref, image_ref, own_w, other_w, norm_ref, middle_ref, second_ref
):
    core = core_ref[0]
    here, there = (pl.multiple_of(HALF * c, LANES) for c in (core, 1 - core))
    for columns, w in ((here, own_w), (there, other_w)):
        middle_ref[:, pl.ds(columns, HALF)] = dot(
            mine_ref[...], w[pl.ds(here, HALF), :], NN
        ) + dot(other_ref[...], w[pl.ds(there, HALF), :], NN)
    middle = image_ref[...].astype(f32) + middle_ref[...] + norm_ref[2:3]
    middle_ref[...] = middle
    second, _, _ = norm_forward(middle, norm_ref[0:1], norm_ref[1:2])
    second_ref[...] = second.astype(bf16)


def middle_call(core, mine, other, image, own_w, other_w, norms):
    vmem = pl.BlockSpec(memory_space=pltpu.VMEM)
    return pl.pallas_call(
        middle_kernel,
        out_shape=(
            jax.ShapeDtypeStruct((TOKENS, D), f32),
            jax.ShapeDtypeStruct((TOKENS, D), bf16),
        ),
        in_specs=[pl.BlockSpec(memory_space=pltpu.SMEM)] + [vmem] * 6,
        out_specs=(vmem,) * 2,
        compiler_params=pltpu.CompilerParams(vmem_limit_bytes=32 * 1024 * 1024),
        cost_estimate=pl.CostEstimate(
            flops=250_000_000, bytes_accessed=3_500_000, transcendentals=0
        ),
    )(core, mine, other, image, own_w, other_w, norms)


def middle_back_kernel(
    core_ref,
    back0_ref,
    back1_ref,
    back2_ref,
    back3_ref,
    second_ref,
    middle_ref,
    dy_ref,
    router_ref,
    own_w,
    other_w,
    norm_ref,
    mine_ref,
    other_ref,
    grad_ref,
    mine_grad_ref,
    other_grad_ref,
    own_cols_ref,
    other_cols_ref,
    vector_ref,
    router_grad_ref,
    total_ref,
    spare_ref,
    codes_ref,
    proj_ref,
):
    core = core_ref[0]
    here, there = (pl.multiple_of(HALF * c, LANES) for c in (core, 1 - core))
    total_ref[...] = (
        back0_ref[...].astype(f32)
        + back1_ref[...].astype(f32)
        + back2_ref[...].astype(f32)
        + back3_ref[...].astype(f32)
    )
    codes_ref[...] = dy_ref[EXTRA:, :SLOTS].astype(f32).astype(jnp.int32)
    lane = lax.broadcasted_iota(jnp.int32, (TOKENS, LANES), 1)
    real = lax.broadcasted_iota(jnp.int32, (TOKENS, D), 0) < PATCHES
    second = second_ref[...]
    gates = find_gates(second, router_ref[...], codes_ref)
    spare_ref[...] = jnp.zeros_like(spare_ref)
    spare = total_ref[EXTRA:, : 2 * LANES]
    spare_ref[:8] = spare + pltpu.roll(spare, 4, 0)
    gate_grad = jnp.where(lane < EXPERTS, spare_ref[...].T[:TOKENS], 0.0)
    mean = jnp.sum(gates * gate_grad, axis=1, keepdims=True)
    logit_grad = (gates * (gate_grad - mean)).astype(bf16)
    second_grad = total_ref[...] + dot(logit_grad, router_ref[...], NT)
    second_grad = jnp.where(real, second_grad, 0.0)
    router_grad_ref[...] = dot(second, logit_grad, TN)
    _, unit, inverse = norm_forward(middle_ref[...], norm_ref[0:1], norm_ref[1:2])
    back, gain_grad, bias_grad = norm_backward(second_grad, unit, inverse, norm_ref[0:1])
    middle_grad = jnp.where(real, dy_ref[...].astype(f32) + back, 0.0)
    grad_ref[...] = middle_grad
    vector_ref[...] = jnp.zeros_like(vector_ref)
    vector_ref[0:1] = gain_grad[None]
    vector_ref[1:2] = bias_grad[None]
    vector_ref[2:3] = jnp.sum(middle_grad, axis=0)[None]
    proj_ref[...] = middle_grad.astype(bf16)
    own = proj_ref[:, pl.ds(here, HALF)]
    other = proj_ref[:, pl.ds(there, HALF)]
    for rows, out_ref in ((here, mine_grad_ref), (there, other_grad_ref)):
        out_ref[...] = (
            dot(own, own_w[pl.ds(rows, HALF), :], NT) + dot(other, other_w[pl.ds(rows, HALF), :], NT)
        ).astype(bf16)
    for columns, out_ref in ((own, own_cols_ref), (other, other_cols_ref)):
        out_ref[pl.ds(here, HALF), :] = dot(mine_ref[...], columns, TN).astype(bf16)
        out_ref[pl.ds(there, HALF), :] = dot(other_ref[...], columns, TN).astype(bf16)


def middle_back_call(after, core, *operands):
    vmem = pl.BlockSpec(memory_space=pltpu.VMEM)
    return pl.pallas_call(
        follow(middle_back_kernel, len(after), 1 + len(operands)),
        out_shape=(
            jax.ShapeDtypeStruct((TOKENS, D), f32),
            jax.ShapeDtypeStruct((TOKENS, HALF), bf16),
            jax.ShapeDtypeStruct((TOKENS, HALF), bf16),
            jax.ShapeDtypeStruct((D, HALF), bf16),
            jax.ShapeDtypeStruct((D, HALF), bf16),
            jax.ShapeDtypeStruct((8, D), f32),
            jax.ShapeDtypeStruct((D, LANES), f32),
        ),
        in_specs=[pl.BlockSpec(memory_space=pltpu.SMEM)]
        + [vmem] * len(operands)
        + [pl.BlockSpec(memory_space=pl.ANY)] * len(after),
        out_specs=(vmem,) * 7,
        scratch_shapes=[
            pltpu.VMEM((TOKENS, D), f32),
            pltpu.VMEM((LANES, 2 * LANES), f32),
            pltpu.VMEM((TOKENS - EXTRA, SLOTS), jnp.int32),
            pltpu.VMEM((TOKENS, D), bf16),
        ],
        compiler_params=pltpu.CompilerParams(vmem_limit_bytes=48 * 1024 * 1024),
        cost_estimate=pl.CostEstimate(
            flops=800_000_000, bytes_accessed=8_000_000, transcendentals=0
        ),
    )(core, *operands, *after)


def follow(kernel, count, n_in):
    def wrapped(*refs):
        return kernel(*refs[:n_in], *refs[n_in + count :])

    return wrapped


def last_kernel(own_ref, arrived_ref, image_ref, norm_ref, middle_grad_ref, grad_ref, vector_ref):
    incoming = own_ref[...] + arrived_ref[...].astype(f32)
    real = lax.broadcasted_iota(jnp.int32, (TOKENS, D), 0) < PATCHES
    incoming = jnp.where(real, incoming, 0.0)
    _, unit, inverse = norm_forward(image_ref[...].astype(f32), norm_ref[0:1], norm_ref[1:2])
    back, gain_grad, bias_grad = norm_backward(incoming, unit, inverse, norm_ref[0:1])
    grad_ref[...] = (middle_grad_ref[...] + back).astype(bf16)
    vector_ref[...] = jnp.zeros_like(vector_ref)
    vector_ref[0:1] = gain_grad[None]
    vector_ref[1:2] = bias_grad[None]


def last_call(after, *operands):
    vmem = pl.BlockSpec(memory_space=pltpu.VMEM)
    return pl.pallas_call(
        follow(last_kernel, len(after), len(operands)),
        out_shape=(
            jax.ShapeDtypeStruct((TOKENS, D), bf16),
            jax.ShapeDtypeStruct((8, D), f32),
        ),
        in_specs=[vmem] * len(operands) + [pl.BlockSpec(memory_space=pl.ANY)] * len(after),
        out_specs=(vmem,) * 2,
        compiler_params=pltpu.CompilerParams(vmem_limit_bytes=24 * 1024 * 1024),
        cost_estimate=pl.CostEstimate(flops=2_000_000, bytes_accessed=2_500_000, transcendentals=0),
    )(*operands, *after)


def image_kernel(
    expert_ref,
    second_ref,
    dy_ref,
    router_ref,
    own_in_ref,
    other_in_ref,
    own_back_ref,
    other_back_ref,
    back_ref,
    mix_ref,
    rows_ref,
    grads_ref,
    active_ref,
    hidden_grad_ref,
    back_sum,
    gate_sum,
    mix_sum,
    codes_ref,
):
    lane = lax.broadcasted_iota(jnp.int32, (TOKENS, LANES), 1)
    token = lax.broadcasted_iota(jnp.int32, (TOKENS, SLOTS), 0)
    codes_ref[...] = dy_ref[EXTRA:, :SLOTS].astype(f32).astype(jnp.int32)
    gates = find_gates(second_ref[...], router_ref[...], codes_ref)
    gate_sum[...] = jnp.zeros_like(gate_sum)
    for k in range(BLOCKS):
        expert = expert_ref[k]
        w_in = block_weight((own_in_ref, other_in_ref), k)
        w_back = block_weight((own_back_ref, other_back_ref), k)
        placing = (token == codes_ref[pl.ds(expert, 1), :]).astype(f32).astype(bf16)
        gate = jnp.sum(jnp.where(lane == expert, gates, 0.0), axis=1, keepdims=True)
        rows = dot(placing, second_ref[...], TN).astype(bf16)
        scaled = (dy_ref[...].astype(f32) * gate).astype(bf16)
        grads = dot(placing, scaled, TN).astype(bf16)
        rows_ref[k] = rows
        grads_ref[k] = grads
        hidden = dot(rows, w_in, NT)
        phi = 0.5 * (1.0 + lax.erf(hidden * (1.0 / math.sqrt(2.0))))
        active = (hidden * phi).astype(bf16)
        slope = phi + hidden * jnp.exp(-0.5 * hidden * hidden) * (1.0 / math.sqrt(2.0 * math.pi))
        active_ref[k] = active
        hidden_grad = (dot(grads, w_back, NT) * slope).astype(bf16)
        hidden_grad_ref[k] = hidden_grad
        produced = dot(active, w_back, NN).astype(bf16)
        rows_grad = dot(hidden_grad, w_in, NN).astype(bf16)
        output = dot(placing, produced, NN)
        gate_grad = jnp.sum(output * dy_ref[...].astype(f32), axis=1, keepdims=True)
        gate_sum[:TOKENS] += jnp.where(lane == expert, gate_grad, 0.0)
        if k == 0:
            back_sum[...] = dot(placing, rows_grad, NN)
            mix_sum[...] = output * gate
        else:
            back_sum[...] += dot(placing, rows_grad, NN)
            mix_sum[...] += output * gate
    spare = gate_sum[...].T[:8]
    high = spare.astype(bf16).astype(f32)
    low = (spare - high).astype(bf16).astype(f32)
    row = lax.broadcasted_iota(jnp.int32, spare.shape, 0)
    back_sum[EXTRA:, : 2 * LANES] = jnp.where(row < 4, high, pltpu.roll(low, 4, 0))
    back_ref[...] = back_sum[...].astype(bf16)
    mix_ref[...] = mix_sum[...].astype(bf16)


def image_call(after, experts, second, dy, router, *weights):
    vmem = pl.BlockSpec(memory_space=pltpu.VMEM)
    return pl.pallas_call(
        follow(image_kernel, len(after), 8),
        out_shape=(
            jax.ShapeDtypeStruct((TOKENS, D), bf16),
            jax.ShapeDtypeStruct((TOKENS, D), bf16),
            jax.ShapeDtypeStruct((BLOCKS, SLOTS, D), bf16),
            jax.ShapeDtypeStruct((BLOCKS, SLOTS, D), bf16),
            jax.ShapeDtypeStruct((BLOCKS, SLOTS, WIDE), bf16),
            jax.ShapeDtypeStruct((BLOCKS, SLOTS, WIDE), bf16),
        ),
        in_specs=[pl.BlockSpec(memory_space=pltpu.SMEM)]
        + [vmem] * 7
        + [pl.BlockSpec(memory_space=pl.ANY)] * len(after),
        out_specs=(vmem,) * 6,
        scratch_shapes=[
            pltpu.VMEM((TOKENS, D), f32),
            pltpu.VMEM((2 * LANES, LANES), f32),
            pltpu.VMEM((TOKENS, D), f32),
            pltpu.VMEM((TOKENS - EXTRA, SLOTS), jnp.int32),
        ],
        compiler_params=pltpu.CompilerParams(vmem_limit_bytes=48 * 1024 * 1024),
        cost_estimate=pl.CostEstimate(
            flops=1, bytes_accessed=1, transcendentals=0
        ),
    )(experts, second, dy, router, *weights, *after)


def weight_kernel(*refs):
    lefts, rights, outs = refs[:ZS], refs[ZS : 2 * ZS], refs[2 * ZS :]
    for half, out_ref in zip((1, 0), outs):
        span = slice(half * WIDE // 2, (half + 1) * WIDE // 2)
        for k in range(BLOCKS):
            total = dot(lefts[0][k, :, span], rights[0][k], TN)
            for n in range(1, ZS):
                total += dot(lefts[n][k, :, span], rights[n][k], TN)
            done = 0
            for x in range(2):
                for y, a, b in block_rows(k):
                    out_ref[y, x, a:b] = total[done : done + b - a].astype(bf16)
                    done += b - a


def weight_call(after, *operands):
    vmem = pl.BlockSpec(memory_space=pltpu.VMEM)
    return pl.pallas_call(
        follow(weight_kernel, len(after), len(operands)),
        out_shape=(jax.ShapeDtypeStruct((2, 2, PIECE_ROWS, D), bf16),) * 2,
        in_specs=[vmem] * len(operands) + [pl.BlockSpec(memory_space=pl.ANY)] * len(after),
        out_specs=(vmem,) * 2,
        compiler_params=pltpu.CompilerParams(vmem_limit_bytes=48 * 1024 * 1024),
        cost_estimate=pl.CostEstimate(
            flops=4_100_000_000, bytes_accessed=9_000_000, transcendentals=0
        ),
    )(*operands, *after)


def pick(value, index, axis=0):
    return lax.dynamic_index_in_dim(value, index, axis, keepdims=False)


def add_rows(kept, got):
    return (kept.astype(f32) + got.astype(f32)).astype(bf16)


def scatter_parts(place, value):
    m = place.teams
    value = value.reshape(4, 2, m, 2, 2 * D // (TEAM * m), -1)
    return value.transpose(0, 1, 3, 2, 4, 5).reshape(4, 2, 2, 2 * D // TEAM, -1)


def scatter_rows(place, left, right, held):
    m = place.teams
    each = D // (TEAM * m)

    def fold(part, axis, side):
        here, move = (place.x, (0, 1)) if axis == "x" else (place.y, (1, 0))
        return add_rows(pick(part, here, side), place.flip(pick(part, 1 - here, side), *move))

    right = fold(scatter_parts(place, right), "y", 1)
    left, right, held = lax.optimization_barrier((left, right, held))
    left, right = fold(left, "y", 1), fold(right, "x", 1)
    both = jnp.concatenate([left, right], axis=-1)
    total = pick(both, place.z).astype(f32)
    for k in range(1, ZS):
        total += place.roll(pick(both, (place.z + k) % ZS), k).astype(f32)
    total = total.reshape(m, 2 * each, -1)
    if m > 1:
        total = lax.psum_scatter(
            total, "fsdp", scatter_dimension=0, axis_index_groups=place.team_groups()
        )
    return total.reshape(2, each, -1), held


def in_order(index, mine, other, axis):
    first = index == 0
    return jnp.stack([jnp.where(first, mine, other), jnp.where(first, other, mine)], axis=axis)


def by_core(place, mine, other):
    first = place.core == 0
    return jnp.stack([jnp.where(first, mine, other), jnp.where(first, other, mine)], axis=-2)


def local(images, slots, small_params, qkv_weight, out_weight, expert_in, expert_out, cotangent):
    place = Place()
    teams = place.teams
    each = D // (TEAM * teams)
    core = place.core
    qkv_rows = qkv_weight.reshape(each, 3, 2, HALF)
    out_rows = out_weight.reshape(each, 2, HALF)
    small_rows = jnp.pad(small_params.reshape(each, 8), ((0, 0), (0, LANES - 8)))

    def half_rows(c):
        return jnp.concatenate(
            [pick(qkv_rows, c, 2).reshape(each, 3 * HALF), small_rows, pick(out_rows, c, 1)], axis=1
        )

    layer = in_order(core, half_rows(core), place.swap_core(half_rows(1 - core)), 0)
    layer = lax.all_gather(
        layer.reshape(2 * each, -1),
        "fsdp",
        axis=0,
        tiled=True,
        axis_index_groups=[list(range(c, teams * TEAM, 2)) for c in range(2)],
    )
    piece_in, piece_back = expert_in.reshape(-1, D), expert_out.reshape(-1, D)
    if teams > 1:
        piece_in, piece_back = (
            lax.all_gather(
                piece, "fsdp", axis=0, tiled=True, axis_index_groups=place.team_groups()
            )
            for piece in (piece_in, piece_back)
        )

    codes = jnp.where(slots[0] >= 0, slots[0] // 2, -1)
    dy_own = jnp.pad(cotangent[0], ((0, EXTRA - PATCHES), (0, 0)))
    spare = jnp.pad(
        codes, ((0, TOKENS - EXTRA - EXPERTS), (0, D - CAP)), constant_values=-1
    ).astype(bf16)
    dy_own = jnp.concatenate([dy_own, spare], axis=0)

    in_parts = turn_send(place, piece_in)
    dy_own, in_parts = lax.optimization_barrier((dy_own, in_parts))
    dy_moved = {k: place.roll(dy_own, k) if k else dy_own for k in (0, 1, 3, 2)}
    turned = turn_join(place, in_parts)
    moves = ((0, 0), (0, 1), (1, 0), (1, 1))
    weights = ()
    for piece in (turned, piece_back):
        pieces = [place.flip(piece, *move) if any(move) else piece for move in moves]
        if piece is turned:
            pieces, dy_moved = lax.optimization_barrier((pieces, dy_moved))
        own = in_order(place.y, jnp.stack(pieces[:2]), jnp.stack(pieces[2:]), 0)
        weights += (own, place.swap_core(own))

    image = images[0]
    inputs = image.astype(f32)
    pair = jnp.stack([image, place.swap_core(image)])
    pair = jnp.pad(pair, ((0, 0), (0, TOKENS - PATCHES), (0, 0)))
    w_qkv = layer[:, : 3 * HALF]
    small = layer[:, 3 * HALF : 3 * HALF + 8].reshape(-1)
    out_own = layer[:, 3 * HALF + LANES :]
    out_other = place.swap_core(out_own)

    gain_one, bias_one, gain_two, bias_two, bias_out = (
        small[n * D : (n + 1) * D].astype(f32) for n in range(5)
    )
    router = jnp.pad(small[5 * D :].reshape(D, EXPERTS), ((0, 0), (0, LANES - EXPERTS)))
    norms = jnp.stack([gain_one, bias_one])
    first, packed, attended_part = attention_call(pair, norms, w_qkv)
    attended_other = place.swap_core(attended_part[1])
    core_index = core[None].astype(jnp.int32)
    norms_two = jnp.stack([gain_two, bias_two, bias_out])
    middle, second_own = middle_call(
        core_index, attended_part[0], attended_other, pair[0], out_own, out_other, norms_two
    )

    experts = (BLOCKS * place.z + jnp.arange(BLOCKS, dtype=jnp.int32)) // ZS
    moved = {k: place.roll(second_own, k) for k in (1, 3, 2)}
    moved[0] = second_own
    results = {}
    returned = {}
    for k in (0, 1, 3, 2):
        after = [returned[n] for n in list(returned)[:-1][-1:] if n]
        if results:
            after.append(before)
        results[k] = image_call(after, experts, moved[k], dy_moved[k], router, *weights)
        before = results[k][0]
        returned[k] = place.roll(before, -k) if k else before
    rows, grads, active, hidden_grad = zip(*(result[2:] for result in results.values()))

    def chip_sum(other, own):
        return (own.astype(f32) + place.swap_core(other).astype(f32)).astype(bf16)

    def spread(chip):
        here, there = pick(chip, place.y), pick(chip, 1 - place.y)
        return [
            here[0],
            place.flip(here[1], 0, 1),
            place.flip(there[0], 1, 0),
            place.flip(there[1], 1, 1),
        ]

    in_other, in_own = weight_call([], *hidden_grad, *rows)
    back_other, back_own = weight_call([in_own, returned[2]], *active, *grads)
    in_chip = chip_sum(in_other, in_own)
    in_moved = spread(in_chip)
    back_chip = chip_sum(back_other, back_own)
    back_moved = spread(back_chip)
    (
        middle_grad,
        mine_grad,
        other_grad,
        proj_own,
        proj_other,
        vectors,
        router_grad,
    ) = middle_back_call(
        [in_chip, back_chip],
        core_index,
        *returned.values(),
        second_own,
        middle,
        dy_own,
        router,
        out_own,
        out_other,
        norms_two,
        attended_part[0],
        attended_other,
    )
    arrived_grad = place.swap_core(other_grad)
    proj_arrived = place.swap_core(proj_other)

    in_parts = turn_send(place, sum(part.astype(f32) for part in in_moved).astype(bf16))
    first_grad, other_grad, qk_grad, v_grad = attention_back_call(
        in_moved[1:] + back_moved[1:2], packed, mine_grad, arrived_grad, first, w_qkv
    )
    mixed = [results[k][1] for k in range(ZS - 1, -1, -1)]
    mixed = lax.dynamic_slice_in_dim(jnp.stack(mixed + mixed), ZS - 1 - place.z, ZS, 0)
    mixed, v_grad = lax.optimization_barrier((mixed, v_grad))
    mixture = lax.psum_scatter(
        mixed, "fsdp", scatter_dimension=0, axis_index_groups=place.line_groups()
    )
    qk_parts = scatter_parts(place, qk_grad)
    sent, in_parts, back_moved[2:] = lax.optimization_barrier(
        (pick(qk_parts, 1 - place.x, 2), in_parts, back_moved[2:])
    )
    qk_got = place.flip(sent, 0, 1)
    input_grad, vectors_one = last_call(
        [], first_grad, place.swap_core(other_grad), pair[0], norms, middle_grad
    )
    input_grad = input_grad[:PATCHES]
    small_terms = jnp.concatenate(
        [
            vectors_one[:2].reshape(-1),
            vectors[:3].reshape(-1),
            router_grad[:, :EXPERTS].reshape(-1),
        ]
    )
    small_terms = small_terms.astype(bf16).reshape(TEAM * teams, -1)
    length = -(-small_terms.shape[1] // LANES)
    small_terms = jnp.pad(
        small_terms, ((0, 0), (0, length * LANES - small_terms.shape[1]))
    ).reshape(TEAM * teams, length, LANES)
    small_terms = jnp.pad(small_terms, ((0, 0), (0, each - length), (0, 0))).reshape(D, LANES)
    proj_grad = (proj_own.astype(f32) + proj_arrived.astype(f32)).astype(bf16)
    rows, back_moved = scatter_rows(
        place,
        add_rows(pick(qk_parts, place.x, 2), qk_got),
        jnp.concatenate([v_grad, proj_grad, small_terms], axis=1),
        back_moved,
    )
    mine = pick(rows, core)
    other = place.swap_core(pick(rows, 1 - core).astype(bf16)).astype(f32)

    def joined(a, b, count):
        cut = [half[:, a:b].reshape(each, count, -1) for half in (mine, other)]
        return by_core(place, *cut).reshape(-1)

    small_grad = mine[:length, 4 * HALF :] + other[:length, 4 * HALF :]
    small_grad = small_grad.reshape(-1)[: 8 * each]
    qkv_weight_grad = joined(0, 3 * HALF, 3)
    out_weight_grad = joined(3 * HALF, 4 * HALF, 1)
    block_output = (middle + mixture.astype(f32))[:PATCHES].astype(bf16)
    in_grad = turn_join(place, in_parts).astype(f32)
    back_grad = sum(part.astype(f32) for part in back_moved)
    if teams > 1:
        in_grad, back_grad = (
            lax.psum_scatter(
                grad,
                "fsdp",
                scatter_dimension=0,
                tiled=True,
                axis_index_groups=place.team_groups(),
            )
            for grad in (in_grad, back_grad)
        )
    return (
        block_output[None],
        input_grad[None],
        small_grad,
        qkv_weight_grad,
        out_weight_grad,
        in_grad.reshape(-1),
        back_grad.reshape(-1),
    )


def solution(mesh):
    rows = P("fsdp", None, None)
    flat = P("fsdp")
    return jax.shard_map(
        local,
        mesh=mesh,
        in_specs=(rows, rows, flat, flat, flat, flat, flat, rows),
        out_specs=(rows, rows, flat, flat, flat, flat, flat),
        check_vma=False,
    )
```
